256 devices in a mesh: img: 32 (over z_hi, y, core), txt: 8 (over x, z_lo).
Axes of the slice: x: 4, y: 4, z: 8 (z_hi: 4, z_lo: 2; z = z_hi * 2 + z_lo), core: 2. Of those that a mesh axis runs over, the one named last changes fastest.
Arguments:
- image_feats: bfloat16 [20480, 1152], P(('img', 'txt')), may hold values from -0.59765625 to 0.59765625
- text_feats: bfloat16 [20480, 1152], P(('img', 'txt')), may hold values from -0.59765625 to 0.59765625
- image_gain: float32 [1152], replicated, may hold values from 0.5 to 2
- text_gain: float32 [1152], replicated, may hold values from 0.5 to 2
Outputs:
- grad_image: bfloat16 [20480, 1152], P(('img', 'txt'))
- grad_text: bfloat16 [20480, 1152], P(('img', 'txt'))
The draws below stay inside these ranges and needn't reach their ends.
All inputs are finite; a program needn't handle non-finite values.
Results may differ from the reference program's by a relative error of at most 0.007.
Values may be sent and summed in bfloat16 or wider, within the bound.
A program may use at most 64 MiB of HBM per device.

```python
import math
import jax
import jax.numpy as jnp
from jax import lax

D = 1152
PAIRS = 20480


def block_scale(rng, shape, pieces, low, high):
    loudness = 1.0
    for position, blocks in pieces:
        heights = jax.random.uniform(jax.random.fold_in(jax.random.fold_in(rng, 6), position), (blocks,), jnp.float32, low / len(pieces), high / len(pieces))
        loudness = loudness * jnp.repeat(jnp.exp(heights), shape[position] // blocks).reshape((-1,) + (1,) * (len(shape) - 1 - position))
    return loudness


def noise(key, dims, deviation, bound, shards=(), kind=jnp.bfloat16):
    array = deviation * jax.random.normal(key, dims, jnp.float32)
    if shards:
        array = array * block_scale(key, dims, shards, -0.22, 0.18)
    return jnp.clip(array, -bound, bound).astype(kind)


def setup_inputs(seed: int = 0) -> dict:
    keys = jax.random.split(jax.random.key(seed), 5)
    return {
        "image_feats": noise(keys[0], (PAIRS, D), 0.1, 0.59765625, ((0, 256),)),
        "text_feats": noise(keys[1], (PAIRS, D), 0.1, 0.59765625, ((0, 256),)),
        "image_gain": jnp.clip(jnp.exp(jax.random.uniform(keys[2], (D,), jnp.float32, math.log(0.5), math.log(2.0))), 0.5, 2.0),
        "text_gain": jnp.clip(jnp.exp(jax.random.uniform(keys[3], (D,), jnp.float32, math.log(0.5), math.log(2.0))), 0.5, 2.0),
    }


EPSILON = 1e-06
BIAS_VALUE = -8.0

def embedding(feats, gain):
    centre = feats - lax.optimization_barrier(jnp.mean(feats, axis=-1, keepdims=True))
    spread = lax.optimization_barrier(jnp.mean(centre * centre, axis=-1, keepdims=True))
    normed = centre * lax.rsqrt(spread + EPSILON) * gain
    energy = lax.optimization_barrier(jnp.mean(normed * normed, axis=-1, keepdims=True))
    return normed * lax.rsqrt(energy + EPSILON) / math.sqrt(feats.shape[-1])

def reference(image_feats, text_feats, image_gain, text_gain):
    image_unit, image_back = jax.vjp(lambda values: embedding(values, image_gain), image_feats.astype(jnp.float32))
    text_unit, text_back = jax.vjp(lambda values: embedding(values, text_gain), text_feats.astype(jnp.float32))
    image_wide = image_unit.astype(jnp.bfloat16).astype(jnp.float32)
    text_wide = text_unit.astype(jnp.bfloat16).astype(jnp.float32)
    block = math.gcd(PAIRS, 512)
    blocks = PAIRS // block
    logit_scale = 2.0 * math.sqrt(D)
    image_index = jnp.arange(PAIRS, dtype=jnp.int32)

    def absorb_block(d_image, block_index):
        first = (block_index * block).astype(jnp.int32)
        text_block = lax.dynamic_slice_in_dim(text_wide, first, block, 0)
        logits = logit_scale * jnp.dot(text_block, image_wide.T, precision=lax.Precision.HIGHEST) + BIAS_VALUE
        text_index = first + jnp.arange(block, dtype=jnp.int32)
        matches = (text_index[:, None] == image_index[None, :]).astype(jnp.float32)
        weights_tile = (logit_scale * (jax.nn.sigmoid(logits) - matches)).astype(jnp.bfloat16)
        weights_tile = lax.optimization_barrier(weights_tile).astype(jnp.float32)
        text_term = jnp.dot(weights_tile, image_wide, precision=lax.Precision.HIGHEST)
        d_image = d_image + jnp.dot(weights_tile.T, text_block, precision=lax.Precision.HIGHEST)
        return (d_image, text_term)
    d_image, text_terms = lax.scan(absorb_block, jnp.zeros((PAIRS, D), jnp.float32), jnp.arange(blocks, dtype=jnp.int32))
    d_text = text_terms.reshape(PAIRS, D)
    grad_image = image_back(d_image)[0].astype(jnp.bfloat16)
    grad_text = text_back(d_text)[0].astype(jnp.bfloat16)
    return (grad_image, grad_text)
```

```python
import math

import jax
import jax.numpy as jnp
from jax import lax
from jax.experimental import pallas as pl
from jax.experimental.pallas import tpu as pltpu
from jax.sharding import PartitionSpec as P

MESH = pl.DeviceIdType.MESH
EPSILON = 1e-06
BIAS_VALUE = -8.0
ROWS = 80
WIDTH = 1152
TOTAL = 16 * ROWS
SCALE = 2.0 * math.sqrt(WIDTH)
LOG2E = math.log2(math.e)
TILE = 256
F32 = jnp.float32
BF16 = jnp.bfloat16

HALVES = ((0, 48), (48, 32))

T_ORDER = [(dp, dq) for dq in (0, 1, 3, 2) for dp in (0, 1, 3, 2)]
Z_ORDER = (0, 1, -1, 2, -2, 3, -3, 4)


def t_row(dp, dq):
    return T_ORDER.index((dp % 4, dq % 4)) * ROWS


def wrap_z(dz):
    return (dz + 3) % 8 - 3


def i_row(dz, dc):
    return (2 * Z_ORDER.index(wrap_z(dz)) + dc) * ROWS


def mean(values):
    return jnp.sum(values, axis=-1, keepdims=True) * (1.0 / WIDTH)


def embed(feats_ref, gain_ref, normed_ref, r1_ref, r2_ref):
    feats = feats_ref[...].astype(F32)
    centre = feats - mean(feats)
    r1 = lax.rsqrt(mean(centre * centre) + EPSILON)
    normed = centre * r1
    scaled = normed * gain_ref[...]
    r2 = lax.rsqrt(mean(scaled * scaled) + EPSILON)
    normed_ref[...] = normed
    r1_ref[...] = r1
    r2_ref[...] = r2
    return (scaled * (r2 * (1.0 / math.sqrt(WIDTH)))).astype(BF16)


def embed_back(cot, gain_ref, normed_ref, r1_ref, r2_ref):
    normed, r1, r2, gain = normed_ref[...], r1_ref[...], r2_ref[...], gain_ref[...]
    scaled = normed * gain
    d_scaled = (cot - scaled * (r2 * r2 * mean(cot * scaled))) * (r2 * (1.0 / math.sqrt(WIDTH)))
    d_normed = d_scaled * gain
    d_centre = (d_normed - normed * mean(d_normed * normed)) * r1
    return (d_centre - mean(d_centre)).astype(BF16)


class Net:
    def __init__(self, send_sems, recv_sems):
        self.send_sems, self.recv_sems = send_sems, recv_sems
        self.copies = {}
        i, t = lax.axis_index("img"), lax.axis_index("txt")
        c, y, x = i % 2, (i // 2) % 4, t // 2
        z = (i // 8) * 2 + t % 2

        def place(x, y, z, c):
            x, y, z = (x + 4) % 4, (y + 4) % 4, (z + 8) % 8
            return (((z // 2) * 4 + y) * 2 + c, x * 2 + z % 2)

        s = 1 - 2 * c
        self.device = {
            "p+": place(x + (1 - c), y + c, z, c),
            "p-": place(x - (1 - c), y - c, z, c),
            "q+": place(x + c, y + (1 - c), z, c),
            "q-": place(x - c, y - (1 - c), z, c),
            "z+": place(x, y, z + s, c),
            "z-": place(x, y, z - s, c),
            "c": place(x, y, z, 1 - c),
        }

    def greet(self):
        barrier = pltpu.get_barrier_semaphore()
        for device in self.device.values():
            pl.semaphore_signal(barrier, inc=1, device_id=device, device_id_type=MESH)

    def greeted(self):
        pl.semaphore_wait(pltpu.get_barrier_semaphore(), len(self.device))

    def send(self, key, src, dst, way):
        number = len(self.copies)
        assert key not in self.copies
        copy = pltpu.make_async_remote_copy(
            src_ref=src,
            dst_ref=dst,
            send_sem=self.send_sems.at[number],
            recv_sem=self.recv_sems.at[number],
            device_id=self.device[way],
            device_id_type=MESH,
        )
        copy.start()
        self.copies[key] = copy

    def arrived(self, key):
        self.copies[key].wait_recv()

    def finish(self):
        for copy in self.copies.values():
            copy.wait_send()


N_COPIES = 160
T_SLOTS = 16
I_SLOTS = 16


def kernel(
    image_ref, text_ref, image_gain_ref, text_gain_ref, image_out, text_out,
    tbuf, ibuf, w, wt, dtext, dimage, tsend, trecv, isend, irecv, csend, crecv,
    inorm, ir1, ir2, tnorm, tr1, tr2, send_sems, recv_sems,
):
    net = Net(send_sems, recv_sems)
    net.greet()

    def send_t(dp, dq, part, way):
        first, size = part
        step = 1 if way[1] == "+" else -1
        there = (dp - step, dq) if way[0] == "p" else (dp, dq - step)
        there = (there[0] % 4, there[1] % 4)
        net.send(
            ("tg", there, first),
            tbuf.at[pl.ds(t_row(dp, dq) + first, size)],
            tbuf.at[pl.ds(t_row(*there) + first, size)],
            way,
        )

    def wait_t(dp, dq, part):
        net.arrived(("tg", (dp % 4, dq % 4), part[0]))

    def send_z(dz, part, way):
        first, size = part
        there = wrap_z(dz - 1 if way == "z+" else dz + 1)
        net.send(
            ("ig", there, 0, first),
            ibuf.at[pl.ds(i_row(dz, 0) + first, size)],
            ibuf.at[pl.ds(i_row(there, 0) + first, size)],
            way,
        )

    def send_c(dz, part):
        first, size = part
        there = wrap_z(-dz)
        net.send(
            ("ig", there, 1, first),
            ibuf.at[pl.ds(i_row(dz, 0) + first, size)],
            ibuf.at[pl.ds(i_row(there, 1) + first, size)],
            "c",
        )

    def wait_i(dz, dc, part):
        net.arrived(("ig", dz, dc, part[0]))

    def tile(a, b, own=False):
        ta, ib = pl.ds(a * TILE, TILE), pl.ds(b * TILE, TILE)
        if not isinstance(a, int):
            ta = pl.ds(pl.multiple_of(a * TILE, TILE), TILE)
        if not isinstance(b, int):
            ib = pl.ds(pl.multiple_of(b * TILE, TILE), TILE)
        dots = lax.dot_general(
            tbuf[ta, :], ibuf[ib, :], (((1,), (1,)), ((), ())), preferred_element_type=F32
        )
        weights = SCALE / (1.0 + jnp.exp2(dots * (-SCALE * LOG2E) - BIAS_VALUE * LOG2E))
        if own:
            row = lax.broadcasted_iota(jnp.int32, (TILE, TILE), 0)
            column = lax.broadcasted_iota(jnp.int32, (TILE, TILE), 1)
            weights = weights - jnp.where((row == column) & (row < ROWS), SCALE, 0.0)
        w[ta, ib] = weights.astype(BF16)
        wt[ib, ta] = weights.T.astype(BF16)

    def tiles(first_a, first_b, count_a, count_b):
        @pl.loop(0, count_a * count_b)
        def _(k):
            tile(first_a + k // count_b, first_b + k % count_b)

    whole = (0, ROWS)
    tbuf[0:ROWS, :] = embed(text_ref, text_gain_ref, tnorm, tr1, tr2)
    net.greeted()
    for part in HALVES:
        for way in ("p+", "p-", "q+", "q-"):
            send_t(0, 0, part, way)
    ibuf[0:ROWS, :] = embed(image_ref, image_gain_ref, inorm, ir1, ir2)
    for part in HALVES:
        for way in ("z+", "z-"):
            send_z(0, part, way)
    send_c(0, whole)

    for k, part in enumerate(HALVES):
        wait_t(-1, 0, part)
        if k == 0:
            send_t(-1, 0, part, "p+")
        send_t(-1, 0, part, "q+")
        send_t(-1, 0, part, "q-")
        wait_t(1, 0, part)
        if k == 1:
            send_t(1, 0, part, "p-")
        send_t(1, 0, part, "q+")
        send_t(1, 0, part, "q-")
        wait_i(-1, 0, part)
        send_z(-1, part, "z+")
        wait_i(1, 0, part)
        send_z(1, part, "z-")
    send_c(1, whole)
    send_c(-1, whole)
    for k, part in enumerate(HALVES):
        wait_t(0, -1, part)
        send_t(0, -1, part, "q+")
        wait_t(0, 1, part)
        wait_t(2, 0, part)
        send_t(2, 0, part, "q+")
        send_t(2, 0, part, "q-")
        wait_i(-2, 0, part)
        send_z(-2, part, "z+")
        wait_i(2, 0, part)
        send_z(2, part, "z-")
    send_c(2, whole)
    send_c(-2, whole)
    wait_i(0, 1, whole)
    wait_i(1, 1, whole)
    wait_i(-1, 1, whole)
    tile(0, 0, own=True)
    for part in HALVES:
        wait_t(1, -1, part)
        send_t(1, -1, part, "q+")
        wait_t(-1, 1, part)
        send_t(-1, 1, part, "q-")
        wait_t(1, 1, part)
        wait_t(-1, -1, part)
        wait_i(-3, 0, part)
        send_z(-3, part, "z+")
        wait_i(3, 0, part)
    send_c(3, whole)
    send_c(-3, whole)
    wait_i(2, 1, whole)
    wait_i(-2, 1, whole)
    tile(0, 1)
    tile(0, 2)
    for part in HALVES:
        wait_t(2, 1, part)
        send_t(2, 1, part, "q-")
        wait_t(2, -1, part)
    tiles(1, 0, 2, 3)
    for part in HALVES:
        wait_i(4, 0, part)
    send_c(4, whole)
    wait_i(3, 1, whole)
    wait_i(-3, 1, whole)
    tiles(0, 3, 3, 1)
    for part in HALVES:
        for dp in (0, 1, -1, 2):
            wait_t(dp, 2, part)
    tiles(3, 0, 2, 4)
    wait_i(4, 1, whole)
    tiles(0, 4, 5, 1)

    def text_rows(dq):
        rows = pl.ds(t_row(0, dq), 4 * ROWS)
        dtext[rows, :] = jnp.dot(w[rows, :], ibuf[...], preferred_element_type=F32)

    def image_rows(first, count):
        rows = pl.ds(first * ROWS, count * ROWS)
        dimage[rows, :] = jnp.dot(wt[rows, :], tbuf[...], preferred_element_type=F32)

    slots = {}

    def slot(kind, key):
        group = slots.setdefault(kind, {})
        return group.setdefault(key, len(group))

    def reduce_t(dp, dq, part, way, takes):
        first, size = part
        step = 1 if way[1] == "+" else -1
        there = (dp - step, dq) if way[0] == "p" else (dp, dq - step)
        key = (there[0] % 4, there[1] % 4, way)
        total = dtext[pl.ds(t_row(dp, dq) + first, size), :]
        total = taken_t(total, dp, dq, part, takes)
        out = tsend.at[slot("t", key), pl.ds(first, size)]
        out[...] = total.astype(BF16)
        net.send(("tr", key, first), out, trecv.at[slot("t", key), pl.ds(first, size)], way)

    def taken_t(total, dp, dq, part, takes):
        first, size = part
        for way in takes:
            key = (dp % 4, dq % 4, way)
            net.arrived(("tr", key, first))
            total = total + trecv[slot("t", key), pl.ds(first, size), :].astype(F32)
        return total

    def swap(dz):
        out = csend.at[Z_ORDER.index(dz)]
        out[...] = dimage[pl.ds(i_row(dz, 1), ROWS), :].astype(BF16)
        there = Z_ORDER.index(wrap_z(-dz))
        net.send(("cr", wrap_z(-dz)), out, crecv.at[there], "c")

    def swapped(dz):
        net.arrived(("cr", dz))
        rows = pl.ds(i_row(dz, 0), ROWS)
        dimage[rows, :] = dimage[rows, :] + crecv[Z_ORDER.index(dz)].astype(F32)

    def taken_i(total, dz, part, takes):
        first, size = part
        for way in takes:
            key = (dz, way)
            net.arrived(("ir", key, first))
            total = total + irecv[slot("i", key), pl.ds(first, size), :].astype(F32)
        return total

    def reduce_i(dz, part, way, takes):
        first, size = part
        total = taken_i(dimage[pl.ds(i_row(dz, 0) + first, size), :], dz, part, takes)
        key = (wrap_z(dz - 1 if way == "z+" else dz + 1), way)
        out = isend.at[slot("i", key), pl.ds(first, size)]
        out[...] = total.astype(BF16)
        net.send(("ir", key, first), out, irecv.at[slot("i", key), pl.ds(first, size)], way)

    image_rows(10, 6)
    for dz in (4, 3, -3):
        swap(dz)
    text_rows(2)
    for dp, way in ((2, "q+"), (1, "q-"), (0, "q+"), (-1, "q-")):
        reduce_t(dp, 2, whole, way, ())
    for dz in (4, 3, -3):
        swapped(dz)
    for part in HALVES:
        reduce_i(4, part, "z+", ())
        reduce_i(-3, part, "z-", ())
    text_rows(1)
    for dp in (1, -1):
        reduce_t(dp, 1, whole, "q+", ())
    text_rows(-1)
    for dp in (2, 0):
        reduce_t(dp, -1, whole, "q-", ())
    image_rows(6, 4)
    for dz in (2, -2):
        swap(dz)
    reduce_t(2, 1, whole, "q+", ("q+",))
    reduce_t(1, -1, whole, "q-", ("q-",))
    for dz in (2, -2):
        swapped(dz)
    for part in HALVES:
        reduce_i(3, part, "z+", ("z+",))
        reduce_i(-2, part, "z-", ("z-",))
    reduce_t(0, 1, whole, "q+", ("q+",))
    reduce_t(-1, -1, whole, "q-", ("q-",))
    image_rows(2, 4)
    for dz in (1, -1):
        swap(dz)
    text_rows(0)
    for part in HALVES:
        reduce_i(2, part, "z+", ("z+",))
    for dz in (1, -1):
        swapped(dz)
    for part in HALVES:
        reduce_i(-1, part, "z-", ("z-",))
    image_rows(0, 2)
    swap(0)

    def join(dp):
        rows = pl.ds(t_row(dp, 0), ROWS)
        dtext[rows, :] = taken_t(dtext[rows, :], dp, 0, whole, ("q+", "q-"))

    join(2)
    reduce_t(2, 0, HALVES[0], "p+", ())
    reduce_t(2, 0, HALVES[1], "p-", ())
    for part in HALVES:
        reduce_i(1, part, "z+", ("z+",))
    join(1)
    reduce_t(1, 0, HALVES[1], "p+", ())
    join(-1)
    reduce_t(-1, 0, HALVES[0], "p-", ())
    swapped(0)
    join(0)
    reduce_t(1, 0, HALVES[0], "p+", ("p+",))
    reduce_t(-1, 0, HALVES[1], "p-", ("p-",))
    total = dimage[0:ROWS, :]
    sums = [
        taken_i(total[first : first + size], 0, (first, size), ("z-", "z+"))
        for first, size in HALVES
    ]
    image_out[...] = embed_back(
        jnp.concatenate(sums, axis=0), image_gain_ref, inorm, ir1, ir2
    )
    total = dtext[0:ROWS, :]
    sums = [
        taken_t(total[first : first + size], 0, 0, (first, size), ("p+", "p-"))
        for first, size in HALVES
    ]
    text_out[...] = embed_back(jnp.concatenate(sums, axis=0), text_gain_ref, tnorm, tr1, tr2)
    net.finish()


def local(image_feats, text_feats, image_gain, text_gain):
    vmem = pl.BlockSpec(memory_space=pltpu.VMEM)
    block = jax.ShapeDtypeStruct((ROWS, WIDTH), BF16)
    flops = 6 * TOTAL * TOTAL * WIDTH
    return pl.pallas_call(
        kernel,
        out_shape=(block, block),
        in_specs=[vmem] * 4,
        out_specs=(vmem, vmem),
        scratch_shapes=[
            pltpu.VMEM((TOTAL, WIDTH), BF16),
            pltpu.VMEM((TOTAL, WIDTH), BF16),
            pltpu.VMEM((TOTAL, TOTAL), BF16),
            pltpu.VMEM((TOTAL, TOTAL), BF16),
            pltpu.VMEM((TOTAL, WIDTH), F32),
            pltpu.VMEM((TOTAL, WIDTH), F32),
            pltpu.VMEM((T_SLOTS, ROWS, WIDTH), BF16),
            pltpu.VMEM((T_SLOTS, ROWS, WIDTH), BF16),
            pltpu.VMEM((7, ROWS, WIDTH), BF16),
            pltpu.VMEM((7, ROWS, WIDTH), BF16),
            pltpu.VMEM((8, ROWS, WIDTH), BF16),
            pltpu.VMEM((8, ROWS, WIDTH), BF16),
            pltpu.VMEM((ROWS, WIDTH), F32),
            pltpu.VMEM((ROWS, 1), F32),
            pltpu.VMEM((ROWS, 1), F32),
            pltpu.VMEM((ROWS, WIDTH), F32),
            pltpu.VMEM((ROWS, 1), F32),
            pltpu.VMEM((ROWS, 1), F32),
            pltpu.SemaphoreType.DMA((N_COPIES,)),
            pltpu.SemaphoreType.DMA((N_COPIES,)),
        ],
        compiler_params=pltpu.CompilerParams(
            collective_id=0, has_side_effects=True, vmem_limit_bytes=56 * 2**20
        ),
        cost_estimate=pl.CostEstimate(
            flops=flops, bytes_accessed=4 * ROWS * WIDTH * 2, transcendentals=TOTAL * TOTAL
        ),
    )(image_feats, text_feats, image_gain.reshape(1, WIDTH), text_gain.reshape(1, WIDTH))


def solution(mesh):
    placed = (P(("img", "txt"), None), P(("img", "txt"), None), P(), P())
    return jax.shard_map(
        local,
        mesh=mesh,
        in_specs=placed,
        out_specs=(P(("img", "txt"), None), P(("img", "txt"), None)),
        check_vma=False,
    )
```

```python
import math

import jax
import jax.numpy as jnp
from jax import lax
from jax.experimental import pallas as pl
from jax.experimental.pallas import tpu as pltpu
from jax.sharding import PartitionSpec as P

MESH = pl.DeviceIdType.MESH
EPSILON = 1e-06
BIAS_VALUE = -8.0
ROWS = 80
WIDTH = 1152
TOTAL = 16 * ROWS
SCALE = 2.0 * math.sqrt(WIDTH)
LOG2E = math.log2(math.e)
TILE = 256
F32 = jnp.float32
BF16 = jnp.bfloat16

HALVES = ((0, 48), (48, 32))

T_ORDER = [(dp, dq) for dq in (0, 1, 3, 2) for dp in (0, 1, 3, 2)]
Z_ORDER = (0, 1, -1, 2, -2, 3, -3, 4)


def t_row(dp, dq):
    return T_ORDER.index((dp % 4, dq % 4)) * ROWS


def wrap_z(dz):
    return (dz + 3) % 8 - 3


def i_row(dz, dc):
    return (2 * Z_ORDER.index(wrap_z(dz)) + dc) * ROWS


def mean(values):
    return jnp.sum(values, axis=-1, keepdims=True) * (1.0 / WIDTH)


def embed(feats_ref, gain_ref, normed_ref, r1_ref, r2_ref):
    feats = feats_ref[...].astype(F32)
    centre = feats - mean(feats)
    r1 = lax.rsqrt(mean(centre * centre) + EPSILON)
    normed = centre * r1
    scaled = normed * gain_ref[...]
    r2 = lax.rsqrt(mean(scaled * scaled) + EPSILON)
    normed_ref[...] = normed
    r1_ref[...] = r1
    r2_ref[...] = r2
    return (scaled * (r2 * (1.0 / math.sqrt(WIDTH)))).astype(BF16)


def embed_back(cot, gain_ref, normed_ref, r1_ref, r2_ref):
    normed, r1, r2, gain = normed_ref[...], r1_ref[...], r2_ref[...], gain_ref[...]
    scaled = normed * gain
    d_scaled = (cot - scaled * (r2 * r2 * mean(cot * scaled))) * (r2 * (1.0 / math.sqrt(WIDTH)))
    d_normed = d_scaled * gain
    d_centre = (d_normed - normed * mean(d_normed * normed)) * r1
    return (d_centre - mean(d_centre)).astype(BF16)


class Net:
    def __init__(self, send_sems, recv_sems):
        self.send_sems, self.recv_sems = send_sems, recv_sems
        self.copies = {}
        i, t = lax.axis_index("img"), lax.axis_index("txt")
        c, y, x = i % 2, (i // 2) % 4, t // 2
        z = (i // 8) * 2 + t % 2

        def place(x, y, z, c):
            x, y, z = (x + 4) % 4, (y + 4) % 4, (z + 8) % 8
            return (((z // 2) * 4 + y) * 2 + c, x * 2 + z % 2)

        s = 1 - 2 * c
        self.device = {
            "p+": place(x + (1 - c), y + c, z, c),
            "p-": place(x - (1 - c), y - c, z, c),
            "q+": place(x + c, y + (1 - c), z, c),
            "q-": place(x - c, y - (1 - c), z, c),
            "z+": place(x, y, z + s, c),
            "z-": place(x, y, z - s, c),
            "c": place(x, y, z, 1 - c),
        }

    def greet(self):
        barrier = pltpu.get_barrier_semaphore()
        for device in self.device.values():
            pl.semaphore_signal(barrier, inc=1, device_id=device, device_id_type=MESH)

    def greeted(self):
        pl.semaphore_wait(pltpu.get_barrier_semaphore(), len(self.device))

    def send(self, key, src, dst, way):
        number = len(self.copies)
        assert key not in self.copies
        copy = pltpu.make_async_remote_copy(
            src_ref=src,
            dst_ref=dst,
            send_sem=self.send_sems.at[number],
            recv_sem=self.recv_sems.at[number],
            device_id=self.device[way],
            device_id_type=MESH,
        )
        copy.start()
        self.copies[key] = copy

    def arrived(self, key):
        self.copies[key].wait_recv()

    def finish(self):
        for copy in self.copies.values():
            copy.wait_send()


N_COPIES = 111
T_SLOTS = 16
I_SLOTS = 16


def kernel(
    image_ref, text_ref, image_gain_ref, text_gain_ref, image_out, text_out,
    tbuf, ibuf, w, wt, dtext, dimage, tsend, trecv, isend, irecv, csend, crecv,
    inorm, ir1, ir2, tnorm, tr1, tr2, image_in, text_in, image_gain_in, text_gain_in, in_sems,
    send_sems, recv_sems,
):
    net = Net(send_sems, recv_sems)
    staged = [
        pltpu.make_async_copy(source, target, in_sems.at[k])
        for k, (source, target) in enumerate(
            (
                (image_ref, image_in),
                (image_gain_ref, image_gain_in),
                (text_ref, text_in),
                (text_gain_ref, text_gain_in),
            )
        )
    ]
    for copy in staged:
        copy.start()
    net.greet()

    def send_t(dp, dq, part, way):
        first, size = part
        step = 1 if way[1] == "+" else -1
        there = (dp - step, dq) if way[0] == "p" else (dp, dq - step)
        there = (there[0] % 4, there[1] % 4)
        net.send(
            ("tg", there, first),
            tbuf.at[pl.ds(t_row(dp, dq) + first, size)],
            tbuf.at[pl.ds(t_row(*there) + first, size)],
            way,
        )

    def wait_t(dp, dq, part):
        net.arrived(("tg", (dp % 4, dq % 4), part[0]))

    def send_z(dz, part, way):
        first, size = part
        there = wrap_z(dz - 1 if way == "z+" else dz + 1)
        net.send(
            ("ig", there, 0, first),
            ibuf.at[pl.ds(i_row(dz, 0) + first, size)],
            ibuf.at[pl.ds(i_row(there, 0) + first, size)],
            way,
        )

    def send_c(dz, part):
        first, size = part
        there = wrap_z(-dz)
        net.send(
            ("ig", there, 1, first),
            ibuf.at[pl.ds(i_row(dz, 0) + first, size)],
            ibuf.at[pl.ds(i_row(there, 1) + first, size)],
            "c",
        )

    def wait_i(dz, dc, part):
        net.arrived(("ig", dz, dc, part[0]))

    def tile(first_t, count_t, first_i, count_i):
        ts, im = pl.ds(first_t, count_t), pl.ds(first_i, count_i)
        dots = lax.dot_general(
            tbuf[ts, :], ibuf[im, :], (((1,), (1,)), ((), ())), preferred_element_type=F32
        )
        weights = SCALE / (1.0 + jnp.exp2(dots * (-SCALE * LOG2E) - BIAS_VALUE * LOG2E))
        if first_t == 0 and first_i == 0:
            row = lax.broadcasted_iota(jnp.int32, weights.shape, 0)
            column = lax.broadcasted_iota(jnp.int32, weights.shape, 1)
            weights = weights - jnp.where((row == column) & (row < ROWS), SCALE, 0.0)
        weights = weights.astype(BF16)
        w[ts, im] = weights
        wt[im, ts] = weights.T

    whole = (0, ROWS)
    staged[0].wait()
    staged[1].wait()
    ibuf[0:ROWS, :] = embed(image_in, image_gain_in, inorm, ir1, ir2)
    net.greeted()
    for part in HALVES:
        for way in ("z+", "z-"):
            send_z(0, part, way)
    send_c(0, whole)
    staged[2].wait()
    staged[3].wait()
    tbuf[0:ROWS, :] = embed(text_in, text_gain_in, tnorm, tr1, tr2)
    for ways in (("p+", "p-"), ("q+", "q-")):
        for part in HALVES:
            for way in ways:
                send_t(0, 0, part, way)

    for k, part in enumerate(HALVES):
        wait_i(-1, 0, part)
        send_z(-1, part, "z+")
        wait_i(1, 0, part)
        send_z(1, part, "z-")
        wait_t(-1, 0, part)
        if k == 0:
            send_t(-1, 0, part, "p+")
        wait_t(1, 0, part)
        if k == 1:
            send_t(1, 0, part, "p-")
        for dp in (-1, 1):
            send_t(dp, 0, part, "q+")
            send_t(dp, 0, part, "q-")
        send_c(1, part)
        send_c(-1, part)
    for k, part in enumerate(HALVES):
        wait_t(0, -1, part)
        send_t(0, -1, part, "q+")
        wait_t(0, 1, part)
        wait_i(-2, 0, part)
        send_z(-2, part, "z+")
        wait_i(2, 0, part)
        send_z(2, part, "z-")
        wait_t(2, 0, part)
        send_t(2, 0, part, "q+")
        send_t(2, 0, part, "q-")
        send_c(2, part)
        send_c(-2, part)
    wait_i(0, 1, whole)
    for part in HALVES:
        wait_i(1, 1, part)
        wait_i(-1, 1, part)
    tile(0, 256, 0, 256)
    for part in HALVES:
        wait_t(1, -1, part)
        send_t(1, -1, part, "q+")
        wait_t(-1, 1, part)
        send_t(-1, 1, part, "q-")
        wait_i(-3, 0, part)
        send_z(-3, part, "z+")
        wait_i(3, 0, part)
        send_c(3, part)
        send_c(-3, part)
        wait_t(1, 1, part)
        wait_t(-1, -1, part)
    for part in HALVES:
        wait_i(2, 1, part)
        wait_i(-2, 1, part)
    tile(0, 256, 256, 512)
    tile(256, 256, 0, 256)
    for part in HALVES:
        wait_t(2, 1, part)
        send_t(2, 1, part, "q-")
        wait_t(2, -1, part)
    tile(256, 256, 256, 512)
    for part in HALVES:
        wait_i(4, 0, part)
        send_c(4, part)
    tile(512, 256, 0, 768)
    for part in HALVES:
        wait_i(3, 1, part)
        wait_i(-3, 1, part)
    tile(0, 768, 768, 256)
    for part in HALVES:
        wait_i(4, 1, part)
    tile(0, 768, 1024, 256)
    for part in HALVES:
        for dp in (0, 1, -1, 2):
            wait_t(dp, 2, part)
    tile(768, 512, 768, 512)
    tile(768, 512, 0, 256)
    tile(768, 512, 256, 512)

    def text_rows(dq):
        rows = pl.ds(t_row(0, dq), 4 * ROWS)
        dtext[rows, :] = jnp.dot(w[rows, :], ibuf[...], preferred_element_type=F32)

    def image_rows(first, count):
        rows = pl.ds(first * ROWS, count * ROWS)
        dimage[rows, :] = jnp.dot(wt[rows, :], tbuf[...], preferred_element_type=F32)

    slots = {}

    def slot(kind, key):
        group = slots.setdefault(kind, {})
        return group.setdefault(key, len(group))

    def reduce_t(dp, dq, part, way, takes):
        first, size = part
        step = 1 if way[1] == "+" else -1
        there = (dp - step, dq) if way[0] == "p" else (dp, dq - step)
        key = (there[0] % 4, there[1] % 4, way)
        total = dtext[pl.ds(t_row(dp, dq) + first, size), :]
        total = taken_t(total, dp, dq, part, takes)
        out = tsend.at[slot("t", key), pl.ds(first, size)]
        out[...] = total.astype(BF16)
        net.send(("tr", key, first), out, trecv.at[slot("t", key), pl.ds(first, size)], way)

    def taken_t(total, dp, dq, part, takes):
        first, size = part
        for way in takes:
            key = (dp % 4, dq % 4, way)
            net.arrived(("tr", key, first))
            total = total + trecv[slot("t", key), pl.ds(first, size), :].astype(F32)
        return total

    def swap(dz):
        out = csend.at[Z_ORDER.index(dz)]
        out[...] = dimage[pl.ds(i_row(dz, 1), ROWS), :].astype(BF16)
        there = Z_ORDER.index(wrap_z(-dz))
        net.send(("cr", wrap_z(-dz)), out, crecv.at[there], "c")

    def swapped(dz):
        net.arrived(("cr", dz))
        rows = pl.ds(i_row(dz, 0), ROWS)
        dimage[rows, :] = dimage[rows, :] + crecv[Z_ORDER.index(dz)].astype(F32)

    def taken_i(total, dz, part, takes):
        first, size = part
        for way in takes:
            key = (dz, way)
            net.arrived(("ir", key, first))
            total = total + irecv[slot("i", key), pl.ds(first, size), :].astype(F32)
        return total

    def reduce_i(dz, part, way, takes):
        first, size = part
        total = taken_i(dimage[pl.ds(i_row(dz, 0) + first, size), :], dz, part, takes)
        key = (wrap_z(dz - 1 if way == "z+" else dz + 1), way)
        out = isend.at[slot("i", key), pl.ds(first, size)]
        out[...] = total.astype(BF16)
        net.send(("ir", key, first), out, irecv.at[slot("i", key), pl.ds(first, size)], way)

    def join(dp):
        for first, size in HALVES:
            rows = pl.ds(t_row(dp, 0) + first, size)
            dtext[rows, :] = taken_t(dtext[rows, :], dp, 0, (first, size), ("q+", "q-"))

    def pass_t(dp, dq, way, takes=()):
        for part in HALVES:
            reduce_t(dp, dq, part, way, takes)

    def pass_i(dz, way, takes=()):
        for part in HALVES:
            reduce_i(dz, part, way, takes)

    image_rows(10, 6)
    for dz in (4, 3, -3):
        swap(dz)
    text_rows(2)
    for dp, way in ((2, "q+"), (1, "q-"), (0, "q+"), (-1, "q-")):
        pass_t(dp, 2, way)
    swapped(4)
    pass_i(4, "z+")
    swapped(-3)
    pass_i(-3, "z-")
    swapped(3)
    text_rows(1)
    pass_t(1, 1, "q+")
    text_rows(-1)
    pass_t(2, -1, "q-")
    for part in HALVES:
        reduce_t(2, 1, part, "q+", ("q+",))
        reduce_t(1, -1, part, "q-", ("q-",))
    pass_t(-1, 1, "q+")
    pass_t(0, -1, "q-")
    image_rows(6, 4)
    for dz in (2, -2):
        swap(dz)
    text_rows(0)
    pass_i(3, "z+", ("z+",))
    for part in HALVES:
        reduce_t(0, 1, part, "q+", ("q+",))
        reduce_t(-1, -1, part, "q-", ("q-",))
    swapped(-2)
    pass_i(-2, "z-", ("z-",))
    swapped(2)
    image_rows(2, 4)
    for dz in (1, -1):
        swap(dz)
    join(2)
    reduce_t(2, 0, HALVES[0], "p+", ())
    reduce_t(2, 0, HALVES[1], "p-", ())
    pass_i(2, "z+", ("z+",))
    swapped(-1)
    pass_i(-1, "z-", ("z-",))
    swapped(1)
    image_rows(0, 2)
    swap(0)
    join(1)
    reduce_t(1, 0, HALVES[1], "p+", ())
    join(-1)
    reduce_t(-1, 0, HALVES[0], "p-", ())
    pass_i(1, "z+", ("z+",))
    reduce_t(1, 0, HALVES[0], "p+", ("p+",))
    reduce_t(-1, 0, HALVES[1], "p-", ("p-",))
    join(0)
    swapped(0)

    total = dtext[0:ROWS, :]
    sums = [
        taken_t(total[first : first + size], 0, 0, (first, size), ("p+", "p-"))
        for first, size in HALVES
    ]
    text_out[...] = embed_back(jnp.concatenate(sums, axis=0), text_gain_in, tnorm, tr1, tr2)
    total = dimage[0:ROWS, :]
    sums = [
        taken_i(total[first : first + size], 0, (first, size), ("z-", "z+"))
        for first, size in HALVES
    ]
    image_out[...] = embed_back(
        jnp.concatenate(sums, axis=0), image_gain_in, inorm, ir1, ir2
    )
    assert len(net.copies) <= N_COPIES, len(net.copies)
    net.finish()


def local(image_feats, text_feats, image_gain, text_gain):
    vmem = pl.BlockSpec(memory_space=pltpu.VMEM)
    block = pltpu.VMEM((ROWS, WIDTH), BF16)
    flops = 6 * TOTAL * TOTAL * WIDTH
    return pl.pallas_call(
        kernel,
        out_shape=(block, block),
        in_specs=[pl.BlockSpec(memory_space=pl.ANY)] * 4,
        out_specs=(vmem, vmem),
        scratch_shapes=[
            pltpu.VMEM((TOTAL, WIDTH), BF16),
            pltpu.VMEM((TOTAL, WIDTH), BF16),
            pltpu.VMEM((TOTAL, TOTAL), BF16),
            pltpu.VMEM((TOTAL, TOTAL), BF16),
            pltpu.VMEM((TOTAL, WIDTH), F32),
            pltpu.VMEM((TOTAL, WIDTH), F32),
            pltpu.VMEM((T_SLOTS, ROWS, WIDTH), BF16),
            pltpu.VMEM((T_SLOTS, ROWS, WIDTH), BF16),
            pltpu.VMEM((7, ROWS, WIDTH), BF16),
            pltpu.VMEM((7, ROWS, WIDTH), BF16),
            pltpu.VMEM((8, ROWS, WIDTH), BF16),
            pltpu.VMEM((8, ROWS, WIDTH), BF16),
            pltpu.VMEM((ROWS, WIDTH), F32),
            pltpu.VMEM((ROWS, 1), F32),
            pltpu.VMEM((ROWS, 1), F32),
            pltpu.VMEM((ROWS, WIDTH), F32),
            pltpu.VMEM((ROWS, 1), F32),
            pltpu.VMEM((ROWS, 1), F32),
            pltpu.VMEM((ROWS, WIDTH), BF16),
            pltpu.VMEM((ROWS, WIDTH), BF16),
            pltpu.VMEM((WIDTH,), F32),
            pltpu.VMEM((WIDTH,), F32),
            pltpu.SemaphoreType.DMA((4,)),
            pltpu.SemaphoreType.DMA((N_COPIES,)),
            pltpu.SemaphoreType.DMA((N_COPIES,)),
        ],
        compiler_params=pltpu.CompilerParams(
            collective_id=0, has_side_effects=True, vmem_limit_bytes=56 * 2**20
        ),
        cost_estimate=pl.CostEstimate(
            flops=flops, bytes_accessed=4 * ROWS * WIDTH * 2, transcendentals=TOTAL * TOTAL
        ),
    )(image_feats, text_feats, image_gain, text_gain)


def solution(mesh):
    placed = (P(("img", "txt"), None), P(("img", "txt"), None), P(), P())
    return jax.shard_map(
        local,
        mesh=mesh,
        in_specs=placed,
        out_specs=(P(("img", "txt"), None), P(("img", "txt"), None)),
        check_vma=False,
    )
```

```python
import math

import jax
import jax.numpy as jnp
from jax import lax
from jax.experimental import pallas as pl
from jax.experimental.pallas import tpu as pltpu
from jax.sharding import PartitionSpec as P

MESH = pl.DeviceIdType.MESH
EPSILON = 1e-06
BIAS_VALUE = -8.0
ROWS = 80
WIDTH = 1152
TOTAL = 16 * ROWS
SCALE = 2.0 * math.sqrt(WIDTH)
LOG2E = math.log2(math.e)
TILE = 256
F32 = jnp.float32
BF16 = jnp.bfloat16

HALVES = ((0, 48), (48, 32))

T_ORDER = [(dp, dq) for dq in (0, 1, 3, 2) for dp in (0, 1, 3, 2)]
Z_ORDER = (0, 1, -1, 2, -2, 3, -3, 4)


def t_row(dp, dq):
    return T_ORDER.index((dp % 4, dq % 4)) * ROWS


def wrap_z(dz):
    return (dz + 3) % 8 - 3


def i_row(dz, dc):
    return (2 * Z_ORDER.index(wrap_z(dz)) + dc) * ROWS


def mean(values):
    return jnp.sum(values, axis=-1, keepdims=True) * (1.0 / WIDTH)


def embed(feats_ref, gain_ref, normed_ref, r1_ref, r2_ref):
    feats = feats_ref[...].astype(F32)
    centre = feats - mean(feats)
    r1 = lax.rsqrt(mean(centre * centre) + EPSILON)
    normed = centre * r1
    scaled = normed * gain_ref[...]
    r2 = lax.rsqrt(mean(scaled * scaled) + EPSILON)
    normed_ref[...] = normed
    r1_ref[...] = r1
    r2_ref[...] = r2
    return (scaled * (r2 * (1.0 / math.sqrt(WIDTH)))).astype(BF16)


def embed_back(cot, gain_ref, normed_ref, r1_ref, r2_ref):
    normed, r1, r2, gain = normed_ref[...], r1_ref[...], r2_ref[...], gain_ref[...]
    scaled = normed * gain
    d_scaled = (cot - scaled * (r2 * r2 * mean(cot * scaled))) * (r2 * (1.0 / math.sqrt(WIDTH)))
    d_normed = d_scaled * gain
    d_centre = (d_normed - normed * mean(d_normed * normed)) * r1
    return (d_centre - mean(d_centre)).astype(BF16)


class Net:
    def __init__(self, send_sems, recv_sems):
        self.send_sems, self.recv_sems = send_sems, recv_sems
        self.copies = {}
        i, t = lax.axis_index("img"), lax.axis_index("txt")
        c, y, x = i % 2, (i // 2) % 4, t // 2
        z = (i // 8) * 2 + t % 2

        def place(x, y, z, c):
            x, y, z = (x + 4) % 4, (y + 4) % 4, (z + 8) % 8
            return (((z // 2) * 4 + y) * 2 + c, x * 2 + z % 2)

        s = 1 - 2 * c
        self.device = {
            "p+": place(x + (1 - c), y + c, z, c),
            "p-": place(x - (1 - c), y - c, z, c),
            "q+": place(x + c, y + (1 - c), z, c),
            "q-": place(x - c, y - (1 - c), z, c),
            "z+": place(x, y, z + s, c),
            "z-": place(x, y, z - s, c),
            "c": place(x, y, z, 1 - c),
        }

    def greet(self):
        barrier = pltpu.get_barrier_semaphore()
        for device in self.device.values():
            pl.semaphore_signal(barrier, inc=1, device_id=device, device_id_type=MESH)

    def greeted(self):
        pl.semaphore_wait(pltpu.get_barrier_semaphore(), len(self.device))

    def send(self, key, src, dst, way):
        number = len(self.copies)
        assert key not in self.copies
        copy = pltpu.make_async_remote_copy(
            src_ref=src,
            dst_ref=dst,
            send_sem=self.send_sems.at[number],
            recv_sem=self.recv_sems.at[number],
            device_id=self.device[way],
            device_id_type=MESH,
        )
        copy.start()
        self.copies[key] = copy

    def arrived(self, key):
        self.copies[key].wait_recv()

    def finish(self):
        for copy in self.copies.values():
            copy.wait_send()


N_COPIES = 111
T_SLOTS = 16
I_SLOTS = 16


def kernel(
    image_ref, text_ref, image_gain_ref, text_gain_ref, image_out, text_out,
    tbuf, ibuf, w, wt, dtext, dimage, tsend, trecv, isend, irecv, csend, crecv,
    inorm, ir1, ir2, tnorm, tr1, tr2, image_in, text_in, image_gain_in, text_gain_in, in_sems,
    send_sems, recv_sems,
):
    net = Net(send_sems, recv_sems)
    staged = [
        pltpu.make_async_copy(source, target, in_sems.at[k])
        for k, (source, target) in enumerate(
            (
                (image_ref, image_in),
                (image_gain_ref, image_gain_in),
                (text_ref, text_in),
                (text_gain_ref, text_gain_in),
            )
        )
    ]
    for copy in staged:
        copy.start()
    net.greet()

    def send_t(dp, dq, part, way):
        first, size = part
        step = 1 if way[1] == "+" else -1
        there = (dp - step, dq) if way[0] == "p" else (dp, dq - step)
        there = (there[0] % 4, there[1] % 4)
        net.send(
            ("tg", there, first),
            tbuf.at[pl.ds(t_row(dp, dq) + first, size)],
            tbuf.at[pl.ds(t_row(*there) + first, size)],
            way,
        )

    def wait_t(dp, dq, part):
        net.arrived(("tg", (dp % 4, dq % 4), part[0]))

    def send_z(dz, part, way):
        first, size = part
        there = wrap_z(dz - 1 if way == "z+" else dz + 1)
        net.send(
            ("ig", there, 0, first),
            ibuf.at[pl.ds(i_row(dz, 0) + first, size)],
            ibuf.at[pl.ds(i_row(there, 0) + first, size)],
            way,
        )

    def send_c(dz, part):
        first, size = part
        there = wrap_z(-dz)
        net.send(
            ("ig", there, 1, first),
            ibuf.at[pl.ds(i_row(dz, 0) + first, size)],
            ibuf.at[pl.ds(i_row(there, 1) + first, size)],
            "c",
        )

    def wait_i(dz, dc, part):
        net.arrived(("ig", dz, dc, part[0]))

    def tile(first_t, count_t, first_i, count_i):
        ts, im = pl.ds(first_t, count_t), pl.ds(first_i, count_i)
        dots = lax.dot_general(
            tbuf[ts, :], ibuf[im, :], (((1,), (1,)), ((), ())), preferred_element_type=F32
        )
        weights = SCALE / (1.0 + jnp.exp2(dots * (-SCALE * LOG2E) - BIAS_VALUE * LOG2E))
        if first_t == 0 and first_i == 0:
            row = lax.broadcasted_iota(jnp.int32, weights.shape, 0)
            column = lax.broadcasted_iota(jnp.int32, weights.shape, 1)
            weights = weights - jnp.where((row == column) & (row < ROWS), SCALE, 0.0)
        weights = weights.astype(BF16)
        w[ts, im] = weights
        wt[im, ts] = weights.T

    def text_rows(first, count, first_k=0, count_k=TOTAL, add=False):
        rows, ks = pl.ds(first, count), pl.ds(first_k, count_k)
        part = jnp.dot(w[rows, ks], ibuf[ks, :], preferred_element_type=F32)
        dtext[rows, :] = dtext[rows, :] + part if add else part

    def image_rows(first, count, first_k=0, count_k=TOTAL, add=False):
        rows, ks = pl.ds(first, count), pl.ds(first_k, count_k)
        part = jnp.dot(wt[rows, ks], tbuf[ks, :], preferred_element_type=F32)
        dimage[rows, :] = dimage[rows, :] + part if add else part

    whole = (0, ROWS)

    def own_image():
        staged[0].wait()
        staged[1].wait()
        ibuf[0:ROWS, :] = embed(image_in, image_gain_in, inorm, ir1, ir2)
        net.greeted()
        for part in HALVES:
            for way in ("z+", "z-"):
                send_z(0, part, way)
        send_c(0, whole)

    def own_text():
        staged[2].wait()
        staged[3].wait()
        tbuf[0:ROWS, :] = embed(text_in, text_gain_in, tnorm, tr1, tr2)
        for ways in (("p+", "p-"), ("q+", "q-")):
            for part in HALVES:
                for way in ways:
                    send_t(0, 0, part, way)

    def hop_image(dz, k):
        part = HALVES[k]
        wait_i(dz, 0, part)
        if dz in (-1, -2, -3):
            send_z(dz, part, "z+")
        if dz in (1, 2):
            send_z(dz, part, "z-")
        send_c(dz, part)

    def hop_text(dp, dq, k):
        part = HALVES[k]
        wait_t(dp, dq, part)
        if dq == 0:
            if dp == -1 and k == 0:
                send_t(dp, dq, part, "p+")
            if dp == 1 and k == 1:
                send_t(dp, dq, part, "p-")
            send_t(dp, dq, part, "q+")
            send_t(dp, dq, part, "q-")
        elif dq == -1 and dp in (0, 1):
            send_t(dp, dq, part, "q+")
        elif dq == 1 and dp in (-1, 2):
            send_t(dp, dq, part, "q-")

    slots = {}

    def slot(kind, key):
        group = slots.setdefault(kind, {})
        return group.setdefault(key, len(group))

    def reduce_t(dp, dq, part, way, takes):
        first, size = part
        step = 1 if way[1] == "+" else -1
        there = (dp - step, dq) if way[0] == "p" else (dp, dq - step)
        key = (there[0] % 4, there[1] % 4, way)
        total = dtext[pl.ds(t_row(dp, dq) + first, size), :]
        total = taken_t(total, dp, dq, part, takes)
        out = tsend.at[slot("t", key), pl.ds(first, size)]
        out[...] = total.astype(BF16)
        net.send(("tr", key, first), out, trecv.at[slot("t", key), pl.ds(first, size)], way)

    def taken_t(total, dp, dq, part, takes):
        first, size = part
        for way in takes:
            key = (dp % 4, dq % 4, way)
            net.arrived(("tr", key, first))
            total = total + trecv[slot("t", key), pl.ds(first, size), :].astype(F32)
        return total

    def swap(dz):
        out = csend.at[Z_ORDER.index(dz)]
        out[...] = dimage[pl.ds(i_row(dz, 1), ROWS), :].astype(BF16)
        there = Z_ORDER.index(wrap_z(-dz))
        net.send(("cr", wrap_z(-dz)), out, crecv.at[there], "c")

    def swapped(dz):
        net.arrived(("cr", dz))
        rows = pl.ds(i_row(dz, 0), ROWS)
        dimage[rows, :] = dimage[rows, :] + crecv[Z_ORDER.index(dz)].astype(F32)

    def taken_i(total, dz, part, takes):
        first, size = part
        for way in takes:
            key = (dz, way)
            net.arrived(("ir", key, first))
            total = total + irecv[slot("i", key), pl.ds(first, size), :].astype(F32)
        return total

    def reduce_i(dz, part, way, takes):
        first, size = part
        total = taken_i(dimage[pl.ds(i_row(dz, 0) + first, size), :], dz, part, takes)
        key = (wrap_z(dz - 1 if way == "z+" else dz + 1), way)
        out = isend.at[slot("i", key), pl.ds(first, size)]
        out[...] = total.astype(BF16)
        net.send(("ir", key, first), out, irecv.at[slot("i", key), pl.ds(first, size)], way)

    def join(dp, part):
        first, size = part
        rows = pl.ds(t_row(dp, 0) + first, size)
        dtext[rows, :] = taken_t(dtext[rows, :], dp, 0, part, ("q+", "q-"))

    def finish_text():
        total = dtext[0:ROWS, :]
        sums = [
            taken_t(total[first : first + size], 0, 0, (first, size), ("p+", "p-"))
            for first, size in HALVES
        ]
        text_out[...] = embed_back(
            jnp.concatenate(sums, axis=0), text_gain_in, tnorm, tr1, tr2
        )

    def finish_image():
        total = dimage[0:ROWS, :]
        sums = [
            taken_i(total[first : first + size], 0, (first, size), ("z-", "z+"))
            for first, size in HALVES
        ]
        image_out[...] = embed_back(
            jnp.concatenate(sums, axis=0), image_gain_in, inorm, ir1, ir2
        )

    own_image()
    own_text()
    wait_i(0, 1, whole)
    hop_image(-1, 0)
    hop_text(-1, 0, 0)
    hop_text(1, 0, 0)
    hop_image(1, 0)
    wait_i(1, 1, HALVES[0])
    hop_text(1, 0, 1)
    hop_text(-1, 0, 1)
    hop_image(-1, 1)
    wait_i(-1, 1, HALVES[0])
    hop_image(1, 1)
    hop_text(0, -1, 0)
    hop_text(0, 1, 0)
    wait_i(1, 1, HALVES[1])
    hop_text(0, -1, 1)
    hop_text(0, 1, 1)
    hop_image(-2, 0)
    wait_i(-1, 1, HALVES[1])
    hop_text(2, 0, 0)
    hop_text(-1, 1, 0)
    hop_image(2, 0)
    wait_i(2, 1, HALVES[0])
    hop_image(-2, 1)
    hop_text(-1, -1, 0)
    hop_text(1, 1, 0)
    wait_i(-2, 1, HALVES[0])
    hop_image(2, 1)
    hop_text(2, 0, 1)
    tile(0, 256, 0, 256)
    hop_text(1, -1, 0)
    tile(0, 256, 256, 256)
    wait_i(2, 1, HALVES[1])
    hop_text(1, 1, 1)
    hop_text(1, -1, 1)
    hop_image(-3, 0)
    wait_i(-2, 1, HALVES[1])
    tile(0, 256, 512, 256)
    hop_text(-1, 1, 1)
    tile(256, 256, 0, 256)
    hop_text(-1, -1, 1)
    tile(256, 256, 256, 256)
    tile(256, 256, 512, 256)
    hop_image(3, 0)
    hop_text(2, 1, 0)
    wait_i(3, 1, HALVES[0])
    hop_text(0, 2, 0)
    hop_image(-3, 1)
    hop_text(0, 2, 1)
    hop_text(-1, 2, 0)
    hop_image(3, 1)
    wait_i(-3, 1, HALVES[0])
    wait_i(3, 1, HALVES[1])
    tile(256, 256, 768, 256)
    hop_text(2, 1, 1)
    tile(0, 256, 768, 256)
    hop_text(2, -1, 0)
    hop_image(4, 0)
    wait_i(-3, 1, HALVES[1])
    hop_text(-1, 2, 1)
    hop_text(2, -1, 1)
    tile(512, 384, 512, 256)
    tile(512, 384, 768, 256)
    tile(512, 384, 0, 256)
    hop_image(4, 1)
    wait_i(4, 1, HALVES[0])
    hop_text(2, 2, 0)
    tile(512, 384, 256, 256)
    hop_text(1, 2, 0)
    hop_text(1, 2, 1)
    wait_i(4, 1, HALVES[1])
    tile(0, 256, 1024, 256)
    hop_text(2, 2, 1)
    tile(896, 384, 768, 256)
    tile(896, 384, 0, 256)
    tile(896, 384, 256, 256)
    tile(512, 384, 1024, 256)
    tile(256, 256, 1024, 256)
    tile(896, 384, 512, 256)
    tile(896, 384, 1024, 256)
    image_rows(1120, 160)
    swap(4)
    text_rows(960, 320)
    reduce_t(2, 2, HALVES[0], "q+", ())
    reduce_t(2, 2, HALVES[1], "q+", ())
    reduce_t(-1, 2, HALVES[0], "q-", ())
    reduce_t(-1, 2, HALVES[1], "q-", ())
    image_rows(800, 320)
    swap(-3)
    swapped(4)
    reduce_i(4, HALVES[1], "z+", ())
    reduce_i(4, HALVES[0], "z+", ())
    swap(3)
    text_rows(320, 320)
    reduce_t(1, 1, HALVES[1], "q+", ())
    reduce_t(1, 2, HALVES[1], "q-", ())
    reduce_t(1, 2, HALVES[0], "q-", ())
    swapped(3)
    reduce_t(-1, 1, HALVES[0], "q+", ())
    text_rows(640, 320)
    swapped(-3)
    reduce_i(-3, HALVES[1], "z-", ())
    reduce_i(-3, HALVES[0], "z-", ())
    reduce_t(2, -1, HALVES[0], "q-", ())
    reduce_t(2, 1, HALVES[0], "q+", ("q+",))
    reduce_t(2, -1, HALVES[1], "q-", ())
    image_rows(480, 320)
    reduce_t(2, 1, HALVES[1], "q+", ("q+",))
    reduce_i(3, HALVES[1], "z+", ("z+",))
    swap(2)
    reduce_t(0, 2, HALVES[0], "q+", ())
    reduce_t(-1, -1, HALVES[0], "q-", ("q-",))
    reduce_i(3, HALVES[0], "z+", ("z+",))
    text_rows(0, 320)
    reduce_t(1, -1, HALVES[1], "q-", ("q-",))
    reduce_t(1, 1, HALVES[0], "q+", ())
    reduce_t(1, -1, HALVES[0], "q-", ("q-",))
    swapped(-2)
    reduce_t(0, 2, HALVES[1], "q+", ())
    swap(-2)
    reduce_i(-2, HALVES[1], "z-", ("z-",))
    image_rows(160, 320)
    reduce_i(-2, HALVES[0], "z-", ("z-",))
    swap(1)
    reduce_t(-1, -1, HALVES[1], "q-", ("q-",))
    reduce_t(-1, 1, HALVES[1], "q+", ())
    swap(-1)
    swapped(2)
    join(2, HALVES[1])
    join(2, HALVES[0])
    reduce_t(2, 0, HALVES[1], "p-", ())
    reduce_t(2, 0, HALVES[0], "p+", ())
    reduce_i(2, HALVES[1], "z+", ("z+",))
    reduce_t(0, -1, HALVES[1], "q-", ())
    image_rows(0, 160)
    swap(0)
    reduce_t(0, 1, HALVES[0], "q+", ("q+",))
    reduce_t(0, -1, HALVES[0], "q-", ())
    join(-1, HALVES[0])
    swapped(-1)
    reduce_i(2, HALVES[0], "z+", ("z+",))
    swapped(1)
    join(1, HALVES[1])
    reduce_i(-1, HALVES[1], "z-", ("z-",))
    swapped(0)
    reduce_t(0, 1, HALVES[1], "q+", ("q+",))
    join(1, HALVES[0])
    reduce_t(1, 0, HALVES[1], "p+", ())
    reduce_i(-1, HALVES[0], "z-", ("z-",))
    join(-1, HALVES[1])
    reduce_t(-1, 0, HALVES[0], "p-", ())
    reduce_i(1, HALVES[1], "z+", ("z+",))
    reduce_t(-1, 0, HALVES[1], "p-", ("p-",))
    reduce_t(1, 0, HALVES[0], "p+", ("p+",))
    reduce_i(1, HALVES[0], "z+", ("z+",))
    join(0, HALVES[0])
    join(0, HALVES[1])
    finish_text()
    finish_image()
    assert len(net.copies) <= N_COPIES, len(net.copies)
    net.finish()


def local(image_feats, text_feats, image_gain, text_gain):
    vmem = pl.BlockSpec(memory_space=pltpu.VMEM)
    block = pltpu.VMEM((ROWS, WIDTH), BF16)
    flops = 6 * TOTAL * TOTAL * WIDTH
    return pl.pallas_call(
        kernel,
        out_shape=(block, block),
        in_specs=[pl.BlockSpec(memory_space=pl.ANY)] * 4,
        out_specs=(vmem, vmem),
        scratch_shapes=[
            pltpu.VMEM((TOTAL, WIDTH), BF16),
            pltpu.VMEM((TOTAL, WIDTH), BF16),
            pltpu.VMEM((TOTAL, TOTAL), BF16),
            pltpu.VMEM((TOTAL, TOTAL), BF16),
            pltpu.VMEM((TOTAL, WIDTH), F32),
            pltpu.VMEM((TOTAL, WIDTH), F32),
            pltpu.VMEM((T_SLOTS, ROWS, WIDTH), BF16),
            pltpu.VMEM((T_SLOTS, ROWS, WIDTH), BF16),
            pltpu.VMEM((7, ROWS, WIDTH), BF16),
            pltpu.VMEM((7, ROWS, WIDTH), BF16),
            pltpu.VMEM((8, ROWS, WIDTH), BF16),
            pltpu.VMEM((8, ROWS, WIDTH), BF16),
            pltpu.VMEM((ROWS, WIDTH), F32),
            pltpu.VMEM((ROWS, 1), F32),
            pltpu.VMEM((ROWS, 1), F32),
            pltpu.VMEM((ROWS, WIDTH), F32),
            pltpu.VMEM((ROWS, 1), F32),
            pltpu.VMEM((ROWS, 1), F32),
            pltpu.VMEM((ROWS, WIDTH), BF16),
            pltpu.VMEM((ROWS, WIDTH), BF16),
            pltpu.VMEM((WIDTH,), F32),
            pltpu.VMEM((WIDTH,), F32),
            pltpu.SemaphoreType.DMA((4,)),
            pltpu.SemaphoreType.DMA((N_COPIES,)),
            pltpu.SemaphoreType.DMA((N_COPIES,)),
        ],
        compiler_params=pltpu.CompilerParams(
            collective_id=0, has_side_effects=True, vmem_limit_bytes=56 * 2**20
        ),
        cost_estimate=pl.CostEstimate(
            flops=flops, bytes_accessed=4 * ROWS * WIDTH * 2, transcendentals=TOTAL * TOTAL
        ),
    )(image_feats, text_feats, image_gain, text_gain)


def solution(mesh):
    placed = (P(("img", "txt"), None), P(("img", "txt"), None), P(), P())
    return jax.shard_map(
        local,
        mesh=mesh,
        in_specs=placed,
        out_specs=(P(("img", "txt"), None), P(("img", "txt"), None)),
        check_vma=False,
    )
```

```python
import math

import jax
import jax.numpy as jnp
from jax import lax
from jax.experimental import pallas as pl
from jax.experimental.pallas import tpu as pltpu
from jax.sharding import PartitionSpec as P

MESH = pl.DeviceIdType.MESH
EPSILON = 1e-06
BIAS_VALUE = -8.0
ROWS = 80
WIDTH = 1152
TOTAL = 16 * ROWS
SCALE = 2.0 * math.sqrt(WIDTH)
LOG2E = math.log2(math.e)
TILE = 256
F32 = jnp.float32
BF16 = jnp.bfloat16

HALVES = ((0, 48), (48, 32))

T_ORDER = [(dp, dq) for dq in (0, 1, 3, 2) for dp in (0, 1, 3, 2)]
Z_ORDER = (0, 1, -1, 2, -2, 3, -3, 4)


def t_row(dp, dq):
    return T_ORDER.index((dp % 4, dq % 4)) * ROWS


def wrap_z(dz):
    return (dz + 3) % 8 - 3


def i_row(dz, dc):
    return (2 * Z_ORDER.index(wrap_z(dz)) + dc) * ROWS


def mean(values):
    return jnp.sum(values, axis=-1, keepdims=True) * (1.0 / WIDTH)


def embed(feats_ref, gain_ref, normed_ref, r1_ref, r2_ref):
    feats = feats_ref[...].astype(F32)
    centre = feats - mean(feats)
    r1 = lax.rsqrt(mean(centre * centre) + EPSILON)
    normed = centre * r1
    scaled = normed * gain_ref[...]
    r2 = lax.rsqrt(mean(scaled * scaled) + EPSILON)
    normed_ref[...] = normed
    r1_ref[...] = r1
    r2_ref[...] = r2
    return (scaled * (r2 * (1.0 / math.sqrt(WIDTH)))).astype(BF16)


def embed_back(cot, gain_ref, normed_ref, r1_ref, r2_ref):
    normed, r1, r2, gain = normed_ref[...], r1_ref[...], r2_ref[...], gain_ref[...]
    scaled = normed * gain
    d_scaled = (cot - scaled * (r2 * r2 * mean(cot * scaled))) * (r2 * (1.0 / math.sqrt(WIDTH)))
    d_normed = d_scaled * gain
    d_centre = (d_normed - normed * mean(d_normed * normed)) * r1
    return (d_centre - mean(d_centre)).astype(BF16)


class Net:
    def __init__(self, send_sems, recv_sems):
        self.send_sems, self.recv_sems = send_sems, recv_sems
        self.copies = {}
        i, t = lax.axis_index("img"), lax.axis_index("txt")
        c, y, x = i % 2, (i // 2) % 4, t // 2
        z = (i // 8) * 2 + t % 2

        def place(x, y, z, c):
            x, y, z = (x + 4) % 4, (y + 4) % 4, (z + 8) % 8
            return (((z // 2) * 4 + y) * 2 + c, x * 2 + z % 2)

        s = 1 - 2 * c
        self.device = {
            "p+": place(x + (1 - c), y + c, z, c),
            "p-": place(x - (1 - c), y - c, z, c),
            "q+": place(x + c, y + (1 - c), z, c),
            "q-": place(x - c, y - (1 - c), z, c),
            "z+": place(x, y, z + s, c),
            "z-": place(x, y, z - s, c),
            "c": place(x, y, z, 1 - c),
        }

    def greet(self):
        barrier = pltpu.get_barrier_semaphore()
        for device in self.device.values():
            pl.semaphore_signal(barrier, inc=1, device_id=device, device_id_type=MESH)

    def greeted(self):
        pl.semaphore_wait(pltpu.get_barrier_semaphore(), len(self.device))

    def send(self, key, src, dst, way):
        number = len(self.copies)
        assert key not in self.copies
        copy = pltpu.make_async_remote_copy(
            src_ref=src,
            dst_ref=dst,
            send_sem=self.send_sems.at[number],
            recv_sem=self.recv_sems.at[number],
            device_id=self.device[way],
            device_id_type=MESH,
        )
        copy.start()
        self.copies[key] = copy

    def arrived(self, key):
        self.copies[key].wait_recv()

    def finish(self):
        for copy in self.copies.values():
            copy.wait_send()


N_COPIES = 111
T_SLOTS = 16
I_SLOTS = 16


def kernel(
    image_ref, text_ref, image_gain_ref, text_gain_ref, image_out, text_out,
    tbuf, ibuf, w, wt, dtext, dimage, tsend, trecv, isend, irecv, csend, crecv,
    inorm, ir1, ir2, tnorm, tr1, tr2, image_in, text_in, image_gain_in, text_gain_in, in_sems,
    send_sems, recv_sems,
):
    net = Net(send_sems, recv_sems)
    staged = [
        pltpu.make_async_copy(source, target, in_sems.at[k])
        for k, (source, target) in enumerate(
            (
                (image_ref, image_in),
                (image_gain_ref, image_gain_in),
                (text_ref, text_in),
                (text_gain_ref, text_gain_in),
            )
        )
    ]
    for copy in staged:
        copy.start()
    net.greet()

    def send_t(dp, dq, part, way):
        first, size = part
        step = 1 if way[1] == "+" else -1
        there = (dp - step, dq) if way[0] == "p" else (dp, dq - step)
        there = (there[0] % 4, there[1] % 4)
        net.send(
            ("tg", there, first),
            tbuf.at[pl.ds(t_row(dp, dq) + first, size)],
            tbuf.at[pl.ds(t_row(*there) + first, size)],
            way,
        )

    def wait_t(dp, dq, part):
        net.arrived(("tg", (dp % 4, dq % 4), part[0]))

    def send_z(dz, part, way):
        first, size = part
        there = wrap_z(dz - 1 if way == "z+" else dz + 1)
        net.send(
            ("ig", there, 0, first),
            ibuf.at[pl.ds(i_row(dz, 0) + first, size)],
            ibuf.at[pl.ds(i_row(there, 0) + first, size)],
            way,
        )

    def send_c(dz, part):
        first, size = part
        there = wrap_z(-dz)
        net.send(
            ("ig", there, 1, first),
            ibuf.at[pl.ds(i_row(dz, 0) + first, size)],
            ibuf.at[pl.ds(i_row(there, 1) + first, size)],
            "c",
        )

    def wait_i(dz, dc, part):
        net.arrived(("ig", dz, dc, part[0]))

    def tile(first_t, count_t, first_i, count_i):
        ts, im = pl.ds(first_t, count_t), pl.ds(first_i, count_i)
        dots = lax.dot_general(
            tbuf[ts, :], ibuf[im, :], (((1,), (1,)), ((), ())), preferred_element_type=F32
        )
        weights = SCALE / (1.0 + jnp.exp2(dots * (-SCALE * LOG2E) - BIAS_VALUE * LOG2E))
        if first_t == 0 and first_i == 0:
            row = lax.broadcasted_iota(jnp.int32, weights.shape, 0)
            column = lax.broadcasted_iota(jnp.int32, weights.shape, 1)
            weights = weights - jnp.where((row == column) & (row < ROWS), SCALE, 0.0)
        weights = weights.astype(BF16)
        w[ts, im] = weights
        wt[im, ts] = weights.T

    def text_rows(first, count, first_k=0, count_k=TOTAL, add=False):
        rows, ks = pl.ds(first, count), pl.ds(first_k, count_k)
        part = jnp.dot(w[rows, ks], ibuf[ks, :], preferred_element_type=F32)
        dtext[rows, :] = dtext[rows, :] + part if add else part

    def image_rows(first, count, first_k=0, count_k=TOTAL, add=False):
        rows, ks = pl.ds(first, count), pl.ds(first_k, count_k)
        part = jnp.dot(wt[rows, ks], tbuf[ks, :], preferred_element_type=F32)
        dimage[rows, :] = dimage[rows, :] + part if add else part

    whole = (0, ROWS)

    def own_image():
        staged[0].wait()
        staged[1].wait()
        ibuf[0:ROWS, :] = embed(image_in, image_gain_in, inorm, ir1, ir2)
        net.greeted()
        for part in HALVES:
            for way in ("z+", "z-"):
                send_z(0, part, way)
        send_c(0, whole)

    def own_text():
        staged[2].wait()
        staged[3].wait()
        tbuf[0:ROWS, :] = embed(text_in, text_gain_in, tnorm, tr1, tr2)
        for ways in (("p+", "p-"), ("q+", "q-")):
            for part in HALVES:
                for way in ways:
                    send_t(0, 0, part, way)

    def hop_image(dz, k):
        part = HALVES[k]
        wait_i(dz, 0, part)
        if dz in (-1, -2, -3):
            send_z(dz, part, "z+")
        if dz in (1, 2):
            send_z(dz, part, "z-")
        send_c(dz, part)

    def hop_text(dp, dq, k):
        part = HALVES[k]
        wait_t(dp, dq, part)
        if dq == 0:
            if dp == -1 and k == 0:
                send_t(dp, dq, part, "p+")
            if dp == 1 and k == 1:
                send_t(dp, dq, part, "p-")
            send_t(dp, dq, part, "q+")
            send_t(dp, dq, part, "q-")
        elif dq == -1 and dp in (0, 1):
            send_t(dp, dq, part, "q+")
        elif dq == 1 and dp in (-1, 2):
            send_t(dp, dq, part, "q-")

    slots = {}

    def slot(kind, key):
        group = slots.setdefault(kind, {})
        return group.setdefault(key, len(group))

    def reduce_t(dp, dq, part, way, takes):
        first, size = part
        step = 1 if way[1] == "+" else -1
        there = (dp - step, dq) if way[0] == "p" else (dp, dq - step)
        key = (there[0] % 4, there[1] % 4, way)
        total = dtext[pl.ds(t_row(dp, dq) + first, size), :]
        total = taken_t(total, dp, dq, part, takes)
        out = tsend.at[slot("t", key), pl.ds(first, size)]
        out[...] = total.astype(BF16)
        net.send(("tr", key, first), out, trecv.at[slot("t", key), pl.ds(first, size)], way)

    def taken_t(total, dp, dq, part, takes):
        first, size = part
        for way in takes:
            key = (dp % 4, dq % 4, way)
            net.arrived(("tr", key, first))
            total = total + trecv[slot("t", key), pl.ds(first, size), :].astype(F32)
        return total

    def swap(dz):
        out = csend.at[Z_ORDER.index(dz)]
        out[...] = dimage[pl.ds(i_row(dz, 1), ROWS), :].astype(BF16)
        there = Z_ORDER.index(wrap_z(-dz))
        net.send(("cr", wrap_z(-dz)), out, crecv.at[there], "c")

    def swapped(dz):
        net.arrived(("cr", dz))
        rows = pl.ds(i_row(dz, 0), ROWS)
        dimage[rows, :] = dimage[rows, :] + crecv[Z_ORDER.index(dz)].astype(F32)

    def taken_i(total, dz, part, takes):
        first, size = part
        for way in takes:
            key = (dz, way)
            net.arrived(("ir", key, first))
            total = total + irecv[slot("i", key), pl.ds(first, size), :].astype(F32)
        return total

    def reduce_i(dz, part, way, takes):
        first, size = part
        total = taken_i(dimage[pl.ds(i_row(dz, 0) + first, size), :], dz, part, takes)
        key = (wrap_z(dz - 1 if way == "z+" else dz + 1), way)
        out = isend.at[slot("i", key), pl.ds(first, size)]
        out[...] = total.astype(BF16)
        net.send(("ir", key, first), out, irecv.at[slot("i", key), pl.ds(first, size)], way)

    def join(dp, part):
        first, size = part
        rows = pl.ds(t_row(dp, 0) + first, size)
        dtext[rows, :] = taken_t(dtext[rows, :], dp, 0, part, ("q+", "q-"))

    def finish_text():
        total = dtext[0:ROWS, :]
        sums = [
            taken_t(total[first : first + size], 0, 0, (first, size), ("p+", "p-"))
            for first, size in HALVES
        ]
        text_out[...] = embed_back(
            jnp.concatenate(sums, axis=0), text_gain_in, tnorm, tr1, tr2
        )

    def finish_image():
        total = dimage[0:ROWS, :]
        sums = [
            taken_i(total[first : first + size], 0, (first, size), ("z-", "z+"))
            for first, size in HALVES
        ]
        image_out[...] = embed_back(
            jnp.concatenate(sums, axis=0), image_gain_in, inorm, ir1, ir2
        )

    own_image()
    own_text()
    wait_i(0, 1, whole)
    hop_image(-1, 0)
    hop_text(-1, 0, 0)
    hop_text(1, 0, 0)
    hop_image(1, 0)
    hop_text(1, 0, 1)
    hop_text(-1, 0, 1)
    wait_i(1, 1, HALVES[0])
    hop_image(-1, 1)
    hop_image(1, 1)
    hop_text(0, -1, 0)
    hop_text(0, 1, 0)
    wait_i(-1, 1, HALVES[0])
    hop_text(0, -1, 1)
    hop_text(0, 1, 1)
    wait_i(1, 1, HALVES[1])
    hop_image(-2, 0)
    wait_i(-1, 1, HALVES[1])
    hop_text(2, 0, 0)
    hop_text(-1, 1, 0)
    hop_image(2, 0)
    wait_i(2, 1, HALVES[0])
    hop_image(-2, 1)
    hop_text(-1, -1, 0)
    hop_text(1, 1, 0)
    hop_image(2, 1)
    hop_text(2, 0, 1)
    tile(0, 256, 0, 512)
    hop_text(1, -1, 0)
    wait_i(-2, 1, HALVES[0])
    hop_text(1, 1, 1)
    wait_i(2, 1, HALVES[1])
    hop_text(1, -1, 1)
    hop_image(-3, 0)
    hop_text(-1, 1, 1)
    tile(256, 256, 0, 512)
    hop_text(-1, -1, 1)
    wait_i(-2, 1, HALVES[1])
    tile(256, 256, 512, 256)
    tile(0, 256, 512, 256)
    hop_image(3, 0)
    hop_text(2, 1, 0)
    wait_i(3, 1, HALVES[0])
    hop_text(0, 2, 0)
    hop_image(-3, 1)
    hop_text(0, 2, 1)
    hop_text(-1, 2, 0)
    hop_image(3, 1)
    wait_i(-3, 1, HALVES[0])
    hop_text(2, 1, 1)
    wait_i(3, 1, HALVES[1])
    tile(256, 256, 768, 256)
    tile(0, 256, 768, 256)
    hop_image(4, 0)
    hop_text(-1, 2, 1)
    hop_text(2, -1, 0)
    wait_i(-3, 1, HALVES[1])
    hop_text(2, -1, 1)
    tile(512, 384, 768, 256)
    tile(512, 384, 512, 256)
    tile(512, 384, 0, 512)
    hop_image(4, 1)
    hop_text(1, 2, 0)
    hop_text(2, 2, 0)
    wait_i(4, 1, HALVES[0])
    hop_text(1, 2, 1)
    hop_text(2, 2, 1)
    tile(896, 384, 0, 512)
    tile(896, 384, 768, 256)
    tile(896, 384, 512, 256)
    wait_i(4, 1, HALVES[1])
    tile(256, 256, 1024, 256)
    tile(0, 256, 1024, 256)
    tile(512, 384, 1024, 256)
    tile(896, 384, 1024, 256)
    image_rows(1120, 160)
    swap(4)
    text_rows(960, 320)
    reduce_t(-1, 2, HALVES[1], "q-", ())
    reduce_t(1, 2, HALVES[0], "q-", ())
    reduce_t(2, 2, HALVES[0], "q+", ())
    reduce_t(2, 2, HALVES[1], "q+", ())
    image_rows(800, 320)
    swap(3)
    swapped(4)
    reduce_i(4, HALVES[0], "z+", ())
    reduce_t(1, 2, HALVES[1], "q-", ())
    text_rows(320, 320)
    reduce_t(-1, 1, HALVES[0], "q+", ())
    reduce_t(1, 1, HALVES[0], "q+", ())
    reduce_i(4, HALVES[1], "z+", ())
    swap(-3)
    reduce_t(-1, 2, HALVES[0], "q-", ())
    text_rows(640, 320)
    swapped(-3)
    reduce_i(-3, HALVES[1], "z-", ())
    reduce_i(-3, HALVES[0], "z-", ())
    reduce_t(2, -1, HALVES[1], "q-", ())
    reduce_t(2, 1, HALVES[0], "q+", ("q+",))
    reduce_t(2, -1, HALVES[0], "q-", ())
    image_rows(480, 320)
    swapped(3)
    reduce_i(3, HALVES[0], "z+", ("z+",))
    swap(2)
    reduce_t(2, 1, HALVES[1], "q+", ("q+",))
    reduce_t(1, -1, HALVES[1], "q-", ("q-",))
    reduce_t(-1, 1, HALVES[1], "q+", ())
    reduce_t(-1, -1, HALVES[1], "q-", ("q-",))
    text_rows(0, 320)
    reduce_t(-1, -1, HALVES[0], "q-", ("q-",))
    reduce_i(3, HALVES[1], "z+", ("z+",))
    reduce_t(0, 2, HALVES[0], "q+", ())
    reduce_t(0, 2, HALVES[1], "q+", ())
    swap(-2)
    reduce_t(1, -1, HALVES[0], "q-", ("q-",))
    swapped(-2)
    reduce_i(-2, HALVES[1], "z-", ("z-",))
    image_rows(160, 320)
    reduce_i(-2, HALVES[0], "z-", ("z-",))
    swap(1)
    swap(-1)
    reduce_t(1, 1, HALVES[1], "q+", ())
    reduce_t(0, -1, HALVES[0], "q-", ())
    image_rows(0, 160)
    swapped(2)
    join(2, HALVES[1])
    reduce_i(2, HALVES[0], "z+", ("z+",))
    swap(0)
    join(2, HALVES[0])
    reduce_t(2, 0, HALVES[1], "p-", ())
    reduce_t(2, 0, HALVES[0], "p+", ())
    join(-1, HALVES[1])
    reduce_t(0, -1, HALVES[1], "q-", ())
    reduce_i(2, HALVES[1], "z+", ("z+",))
    swapped(-1)
    swapped(1)
    reduce_t(0, 1, HALVES[0], "q+", ("q+",))
    join(-1, HALVES[0])
    reduce_t(-1, 0, HALVES[0], "p-", ())
    reduce_i(-1, HALVES[1], "z-", ("z-",))
    swapped(0)
    reduce_t(0, 1, HALVES[1], "q+", ("q+",))
    join(1, HALVES[0])
    reduce_i(-1, HALVES[0], "z-", ("z-",))
    join(1, HALVES[1])
    reduce_t(1, 0, HALVES[1], "p+", ())
    reduce_i(1, HALVES[0], "z+", ("z+",))
    reduce_t(1, 0, HALVES[0], "p+", ("p+",))
    reduce_t(-1, 0, HALVES[1], "p-", ("p-",))
    reduce_i(1, HALVES[1], "z+", ("z+",))
    join(0, HALVES[0])
    join(0, HALVES[1])
    finish_text()
    finish_image()
    assert len(net.copies) <= N_COPIES, len(net.copies)
    net.finish()


def local(image_feats, text_feats, image_gain, text_gain):
    vmem = pl.BlockSpec(memory_space=pltpu.VMEM)
    block = pltpu.VMEM((ROWS, WIDTH), BF16)
    flops = 6 * TOTAL * TOTAL * WIDTH
    return pl.pallas_call(
        kernel,
        out_shape=(block, block),
        in_specs=[pl.BlockSpec(memory_space=pl.ANY)] * 4,
        out_specs=(vmem, vmem),
        scratch_shapes=[
            pltpu.VMEM((TOTAL, WIDTH), BF16),
            pltpu.VMEM((TOTAL, WIDTH), BF16),
            pltpu.VMEM((TOTAL, TOTAL), BF16),
            pltpu.VMEM((TOTAL, TOTAL), BF16),
            pltpu.VMEM((TOTAL, WIDTH), F32),
            pltpu.VMEM((TOTAL, WIDTH), F32),
            pltpu.VMEM((T_SLOTS, ROWS, WIDTH), BF16),
            pltpu.VMEM((T_SLOTS, ROWS, WIDTH), BF16),
            pltpu.VMEM((7, ROWS, WIDTH), BF16),
            pltpu.VMEM((7, ROWS, WIDTH), BF16),
            pltpu.VMEM((8, ROWS, WIDTH), BF16),
            pltpu.VMEM((8, ROWS, WIDTH), BF16),
            pltpu.VMEM((ROWS, WIDTH), F32),
            pltpu.VMEM((ROWS, 1), F32),
            pltpu.VMEM((ROWS, 1), F32),
            pltpu.VMEM((ROWS, WIDTH), F32),
            pltpu.VMEM((ROWS, 1), F32),
            pltpu.VMEM((ROWS, 1), F32),
            pltpu.VMEM((ROWS, WIDTH), BF16),
            pltpu.VMEM((ROWS, WIDTH), BF16),
            pltpu.VMEM((WIDTH,), F32),
            pltpu.VMEM((WIDTH,), F32),
            pltpu.SemaphoreType.DMA((4,)),
            pltpu.SemaphoreType.DMA((N_COPIES,)),
            pltpu.SemaphoreType.DMA((N_COPIES,)),
        ],
        compiler_params=pltpu.CompilerParams(
            collective_id=0, has_side_effects=True, vmem_limit_bytes=56 * 2**20
        ),
        cost_estimate=pl.CostEstimate(
            flops=flops, bytes_accessed=4 * ROWS * WIDTH * 2, transcendentals=TOTAL * TOTAL
        ),
    )(image_feats, text_feats, image_gain, text_gain)


def solution(mesh):
    placed = (P(("img", "txt"), None), P(("img", "txt"), None), P(), P())
    return jax.shard_map(
        local,
        mesh=mesh,
        in_specs=placed,
        out_specs=(P(("img", "txt"), None), P(("img", "txt"), None)),
        check_vma=False,
    )
```

```python
import math

import jax
import jax.numpy as jnp
from jax import lax
from jax.experimental import pallas as pl
from jax.experimental.pallas import tpu as pltpu
from jax.sharding import PartitionSpec as P

MESH = pl.DeviceIdType.MESH
EPSILON = 1e-06
BIAS_VALUE = -8.0
ROWS = 80
WIDTH = 1152
TOTAL = 16 * ROWS
SCALE = 2.0 * math.sqrt(WIDTH)
LOG2E = math.log2(math.e)
TILE = 256
F32 = jnp.float32
BF16 = jnp.bfloat16

HALVES = ((0, 48), (48, 32))

T_ORDER = [(dp, dq) for dq in (0, 1, 3, 2) for dp in (0, 1, 3, 2)]
Z_ORDER = (0, 1, -1, 2, -2, 3, -3, 4)


def t_row(dp, dq):
    return T_ORDER.index((dp % 4, dq % 4)) * ROWS


def wrap_z(dz):
    return (dz + 3) % 8 - 3


def i_row(dz, dc):
    return (2 * Z_ORDER.index(wrap_z(dz)) + dc) * ROWS


def mean(values):
    return jnp.sum(values, axis=-1, keepdims=True) * (1.0 / WIDTH)


def embed(feats_ref, gain_ref, normed_ref, r1_ref, r2_ref):
    feats = feats_ref[...].astype(F32)
    centre = feats - mean(feats)
    r1 = lax.rsqrt(mean(centre * centre) + EPSILON)
    normed = centre * r1
    scaled = normed * gain_ref[...]
    r2 = lax.rsqrt(mean(scaled * scaled) + EPSILON)
    normed_ref[...] = normed
    r1_ref[...] = r1
    r2_ref[...] = r2
    return (scaled * (r2 * (1.0 / math.sqrt(WIDTH)))).astype(BF16)


def embed_back(cot, gain_ref, normed_ref, r1_ref, r2_ref):
    normed, r1, r2, gain = normed_ref[...], r1_ref[...], r2_ref[...], gain_ref[...]
    scaled = normed * gain
    d_scaled = (cot - scaled * (r2 * r2 * mean(cot * scaled))) * (r2 * (1.0 / math.sqrt(WIDTH)))
    d_normed = d_scaled * gain
    d_centre = (d_normed - normed * mean(d_normed * normed)) * r1
    return (d_centre - mean(d_centre)).astype(BF16)


class Net:
    def __init__(self, send_sems, recv_sems):
        self.send_sems, self.recv_sems = send_sems, recv_sems
        self.copies = {}
        i, t = lax.axis_index("img"), lax.axis_index("txt")
        c, y, x = i % 2, (i // 2) % 4, t // 2
        z = (i // 8) * 2 + t % 2

        def place(x, y, z, c):
            x, y, z = (x + 4) % 4, (y + 4) % 4, (z + 8) % 8
            return (((z // 2) * 4 + y) * 2 + c, x * 2 + z % 2)

        s = 1 - 2 * c
        self.device = {
            "p+": place(x + (1 - c), y + c, z, c),
            "p-": place(x - (1 - c), y - c, z, c),
            "q+": place(x + c, y + (1 - c), z, c),
            "q-": place(x - c, y - (1 - c), z, c),
            "z+": place(x, y, z + s, c),
            "z-": place(x, y, z - s, c),
            "c": place(x, y, z, 1 - c),
        }

    def greet(self):
        barrier = pltpu.get_barrier_semaphore()
        for device in self.device.values():
            pl.semaphore_signal(barrier, inc=1, device_id=device, device_id_type=MESH)

    def greeted(self):
        pl.semaphore_wait(pltpu.get_barrier_semaphore(), len(self.device))

    def send(self, key, src, dst, way):
        number = len(self.copies)
        assert key not in self.copies
        copy = pltpu.make_async_remote_copy(
            src_ref=src,
            dst_ref=dst,
            send_sem=self.send_sems.at[number],
            recv_sem=self.recv_sems.at[number],
            device_id=self.device[way],
            device_id_type=MESH,
        )
        copy.start()
        self.copies[key] = copy

    def arrived(self, key):
        self.copies[key].wait_recv()

    def finish(self):
        for copy in self.copies.values():
            copy.wait_send()


N_COPIES = 111
T_SLOTS = 16
I_SLOTS = 16


def kernel(
    image_ref, text_ref, image_gain_ref, text_gain_ref, image_out, text_out,
    tbuf, ibuf, w, wt, dtext, dimage, tsend, trecv, isend, irecv, csend, crecv,
    inorm, ir1, ir2, tnorm, tr1, tr2, image_in, text_in, image_gain_in, text_gain_in, in_sems,
    send_sems, recv_sems,
):
    net = Net(send_sems, recv_sems)
    staged = [
        pltpu.make_async_copy(source, target, in_sems.at[k])
        for k, (source, target) in enumerate(
            (
                (image_ref, image_in),
                (image_gain_ref, image_gain_in),
                (text_ref, text_in),
                (text_gain_ref, text_gain_in),
            )
        )
    ]
    for copy in staged:
        copy.start()
    net.greet()

    def send_t(dp, dq, part, way):
        first, size = part
        step = 1 if way[1] == "+" else -1
        there = (dp - step, dq) if way[0] == "p" else (dp, dq - step)
        there = (there[0] % 4, there[1] % 4)
        net.send(
            ("tg", there, first),
            tbuf.at[pl.ds(t_row(dp, dq) + first, size)],
            tbuf.at[pl.ds(t_row(*there) + first, size)],
            way,
        )

    def wait_t(dp, dq, part):
        net.arrived(("tg", (dp % 4, dq % 4), part[0]))

    def send_z(dz, part, way):
        first, size = part
        there = wrap_z(dz - 1 if way == "z+" else dz + 1)
        net.send(
            ("ig", there, 0, first),
            ibuf.at[pl.ds(i_row(dz, 0) + first, size)],
            ibuf.at[pl.ds(i_row(there, 0) + first, size)],
            way,
        )

    def send_c(dz, part):
        first, size = part
        there = wrap_z(-dz)
        net.send(
            ("ig", there, 1, first),
            ibuf.at[pl.ds(i_row(dz, 0) + first, size)],
            ibuf.at[pl.ds(i_row(there, 1) + first, size)],
            "c",
        )

    def wait_i(dz, dc, part):
        net.arrived(("ig", dz, dc, part[0]))

    def tile(first_t, count_t, first_i, count_i):
        ts, im = pl.ds(first_t, count_t), pl.ds(first_i, count_i)
        dots = lax.dot_general(
            tbuf[ts, :], ibuf[im, :], (((1,), (1,)), ((), ())), preferred_element_type=F32
        )
        weights = SCALE / (1.0 + jnp.exp2(dots * (-SCALE * LOG2E) - BIAS_VALUE * LOG2E))
        if first_t == 0 and first_i == 0:
            row = lax.broadcasted_iota(jnp.int32, weights.shape, 0)
            column = lax.broadcasted_iota(jnp.int32, weights.shape, 1)
            weights = weights - jnp.where((row == column) & (row < ROWS), SCALE, 0.0)
        weights = weights.astype(BF16)
        w[ts, im] = weights
        wt[im, ts] = weights.T

    def text_rows(first, count, first_k=0, count_k=TOTAL, add=False):
        rows, ks = pl.ds(first, count), pl.ds(first_k, count_k)
        part = jnp.dot(w[rows, ks], ibuf[ks, :], preferred_element_type=F32)
        dtext[rows, :] = dtext[rows, :] + part if add else part

    def image_rows(first, count, first_k=0, count_k=TOTAL, add=False):
        rows, ks = pl.ds(first, count), pl.ds(first_k, count_k)
        part = jnp.dot(wt[rows, ks], tbuf[ks, :], preferred_element_type=F32)
        dimage[rows, :] = dimage[rows, :] + part if add else part

    whole = (0, ROWS)

    def own_image():
        staged[0].wait()
        staged[1].wait()
        ibuf[0:ROWS, :] = embed(image_in, image_gain_in, inorm, ir1, ir2)
        net.greeted()
        for part in HALVES:
            for way in ("z+", "z-"):
                send_z(0, part, way)
        send_c(0, whole)

    def own_text():
        staged[2].wait()
        staged[3].wait()
        tbuf[0:ROWS, :] = embed(text_in, text_gain_in, tnorm, tr1, tr2)
        for ways in (("p+", "p-"), ("q+", "q-")):
            for part in HALVES:
                for way in ways:
                    send_t(0, 0, part, way)

    def hop_image(dz, k):
        part = HALVES[k]
        wait_i(dz, 0, part)
        if dz in (-1, -2, -3):
            send_z(dz, part, "z+")
        if dz in (1, 2):
            send_z(dz, part, "z-")
        send_c(dz, part)

    def hop_text(dp, dq, k):
        part = HALVES[k]
        wait_t(dp, dq, part)
        if dq == 0:
            if dp == -1 and k == 0:
                send_t(dp, dq, part, "p+")
            if dp == 1 and k == 1:
                send_t(dp, dq, part, "p-")
            send_t(dp, dq, part, "q+")
            send_t(dp, dq, part, "q-")
        elif dq == -1 and dp in (0, 1):
            send_t(dp, dq, part, "q+")
        elif dq == 1 and dp in (-1, 2):
            send_t(dp, dq, part, "q-")

    slots = {}

    def slot(kind, key):
        group = slots.setdefault(kind, {})
        return group.setdefault(key, len(group))

    def reduce_t(dp, dq, part, way, takes):
        first, size = part
        step = 1 if way[1] == "+" else -1
        there = (dp - step, dq) if way[0] == "p" else (dp, dq - step)
        key = (there[0] % 4, there[1] % 4, way)
        total = dtext[pl.ds(t_row(dp, dq) + first, size), :]
        total = taken_t(total, dp, dq, part, takes)
        out = tsend.at[slot("t", key), pl.ds(first, size)]
        out[...] = total.astype(BF16)
        net.send(("tr", key, first), out, trecv.at[slot("t", key), pl.ds(first, size)], way)

    def taken_t(total, dp, dq, part, takes):
        first, size = part
        for way in takes:
            key = (dp % 4, dq % 4, way)
            net.arrived(("tr", key, first))
            total = total + trecv[slot("t", key), pl.ds(first, size), :].astype(F32)
        return total

    def swap(dz):
        out = csend.at[Z_ORDER.index(dz)]
        out[...] = dimage[pl.ds(i_row(dz, 1), ROWS), :].astype(BF16)
        there = Z_ORDER.index(wrap_z(-dz))
        net.send(("cr", wrap_z(-dz)), out, crecv.at[there], "c")

    def swapped(dz):
        net.arrived(("cr", dz))
        rows = pl.ds(i_row(dz, 0), ROWS)
        dimage[rows, :] = dimage[rows, :] + crecv[Z_ORDER.index(dz)].astype(F32)

    def taken_i(total, dz, part, takes):
        first, size = part
        for way in takes:
            key = (dz, way)
            net.arrived(("ir", key, first))
            total = total + irecv[slot("i", key), pl.ds(first, size), :].astype(F32)
        return total

    def reduce_i(dz, part, way, takes):
        first, size = part
        total = taken_i(dimage[pl.ds(i_row(dz, 0) + first, size), :], dz, part, takes)
        key = (wrap_z(dz - 1 if way == "z+" else dz + 1), way)
        out = isend.at[slot("i", key), pl.ds(first, size)]
        out[...] = total.astype(BF16)
        net.send(("ir", key, first), out, irecv.at[slot("i", key), pl.ds(first, size)], way)

    def join(dp, part):
        first, size = part
        rows = pl.ds(t_row(dp, 0) + first, size)
        dtext[rows, :] = taken_t(dtext[rows, :], dp, 0, part, ("q+", "q-"))

    def finish_text():
        total = dtext[0:ROWS, :]
        sums = [
            taken_t(total[first : first + size], 0, 0, (first, size), ("p+", "p-"))
            for first, size in HALVES
        ]
        text_out[...] = embed_back(
            jnp.concatenate(sums, axis=0), text_gain_in, tnorm, tr1, tr2
        )

    def finish_image():
        total = dimage[0:ROWS, :]
        sums = [
            taken_i(total[first : first + size], 0, (first, size), ("z-", "z+"))
            for first, size in HALVES
        ]
        image_out[...] = embed_back(
            jnp.concatenate(sums, axis=0), image_gain_in, inorm, ir1, ir2
        )

    own_image()
    own_text()
    wait_i(0, 1, whole)
    hop_image(-1, 0)
    hop_text(-1, 0, 0)
    hop_text(1, 0, 0)
    hop_image(1, 0)
    wait_i(1, 1, HALVES[0])
    hop_text(1, 0, 1)
    hop_text(-1, 0, 1)
    hop_image(-1, 1)
    wait_i(-1, 1, HALVES[0])
    hop_image(1, 1)
    hop_text(0, -1, 0)
    hop_text(0, 1, 0)
    wait_i(1, 1, HALVES[1])
    hop_text(0, -1, 1)
    hop_text(0, 1, 1)
    hop_image(-2, 0)
    wait_i(-1, 1, HALVES[1])
    hop_text(2, 0, 0)
    hop_text(-1, 1, 0)
    hop_image(2, 0)
    wait_i(2, 1, HALVES[0])
    hop_image(-2, 1)
    hop_text(-1, -1, 0)
    hop_text(1, 1, 0)
    wait_i(-2, 1, HALVES[0])
    hop_image(2, 1)
    hop_text(2, 0, 1)
    tile(0, 256, 0, 256)
    hop_text(1, -1, 0)
    tile(0, 256, 256, 256)
    wait_i(2, 1, HALVES[1])
    hop_text(1, 1, 1)
    hop_text(1, -1, 1)
    hop_image(-3, 0)
    wait_i(-2, 1, HALVES[1])
    tile(0, 256, 512, 256)
    hop_text(-1, 1, 1)
    tile(256, 256, 0, 256)
    hop_text(-1, -1, 1)
    tile(256, 256, 256, 256)
    tile(256, 256, 512, 256)
    hop_image(3, 0)
    hop_text(2, 1, 0)
    wait_i(3, 1, HALVES[0])
    hop_text(0, 2, 0)
    hop_image(-3, 1)
    hop_text(0, 2, 1)
    hop_text(-1, 2, 0)
    hop_image(3, 1)
    wait_i(-3, 1, HALVES[0])
    wait_i(3, 1, HALVES[1])
    tile(256, 256, 768, 256)
    hop_text(2, 1, 1)
    tile(0, 256, 768, 256)
    hop_text(2, -1, 0)
    hop_image(4, 0)
    wait_i(-3, 1, HALVES[1])
    hop_text(-1, 2, 1)
    hop_text(2, -1, 1)
    tile(512, 384, 512, 256)
    tile(512, 384, 768, 256)
    tile(512, 384, 0, 256)
    hop_image(4, 1)
    wait_i(4, 1, HALVES[0])
    hop_text(2, 2, 0)
    tile(512, 384, 256, 256)
    hop_text(1, 2, 0)
    hop_text(1, 2, 1)
    wait_i(4, 1, HALVES[1])
    tile(0, 256, 1024, 256)
    hop_text(2, 2, 1)
    tile(896, 384, 768, 256)
    tile(896, 384, 0, 256)
    tile(896, 384, 256, 256)
    tile(512, 384, 1024, 256)
    tile(256, 256, 1024, 256)
    tile(896, 384, 512, 256)
    tile(896, 384, 1024, 256)
    image_rows(1120, 160)
    swap(4)
    text_rows(960, 320)
    reduce_t(2, 2, HALVES[0], "q+", ())
    reduce_t(2, 2, HALVES[1], "q+", ())
    reduce_t(-1, 2, HALVES[0], "q-", ())
    reduce_t(-1, 2, HALVES[1], "q-", ())
    image_rows(800, 320)
    swap(-3)
    swapped(4)
    reduce_i(4, HALVES[1], "z+", ())
    reduce_i(4, HALVES[0], "z+", ())
    swap(3)
    text_rows(320, 320)
    reduce_t(1, 1, HALVES[1], "q+", ())
    reduce_t(1, 2, HALVES[1], "q-", ())
    reduce_t(1, 2, HALVES[0], "q-", ())
    swapped(3)
    reduce_t(-1, 1, HALVES[0], "q+", ())
    text_rows(640, 320)
    swapped(-3)
    reduce_i(-3, HALVES[1], "z-", ())
    reduce_i(-3, HALVES[0], "z-", ())
    reduce_t(2, -1, HALVES[0], "q-", ())
    reduce_t(2, 1, HALVES[0], "q+", ("q+",))
    reduce_t(2, -1, HALVES[1], "q-", ())
    image_rows(480, 320)
    reduce_t(2, 1, HALVES[1], "q+", ("q+",))
    reduce_i(3, HALVES[1], "z+", ("z+",))
    swap(2)
    reduce_t(0, 2, HALVES[0], "q+", ())
    reduce_t(-1, -1, HALVES[0], "q-", ("q-",))
    reduce_i(3, HALVES[0], "z+", ("z+",))
    text_rows(0, 320)
    reduce_t(1, -1, HALVES[1], "q-", ("q-",))
    reduce_t(1, 1, HALVES[0], "q+", ())
    reduce_t(1, -1, HALVES[0], "q-", ("q-",))
    swapped(-2)
    reduce_t(0, 2, HALVES[1], "q+", ())
    swap(-2)
    reduce_i(-2, HALVES[1], "z-", ("z-",))
    image_rows(160, 320)
    reduce_i(-2, HALVES[0], "z-", ("z-",))
    swap(1)
    reduce_t(-1, -1, HALVES[1], "q-", ("q-",))
    reduce_t(-1, 1, HALVES[1], "q+", ())
    swap(-1)
    swapped(2)
    join(2, HALVES[1])
    join(2, HALVES[0])
    reduce_t(2, 0, HALVES[1], "p-", ())
    reduce_t(2, 0, HALVES[0], "p+", ())
    reduce_i(2, HALVES[1], "z+", ("z+",))
    reduce_t(0, -1, HALVES[1], "q-", ())
    image_rows(0, 160)
    swap(0)
    reduce_t(0, 1, HALVES[0], "q+", ("q+",))
    reduce_t(0, -1, HALVES[0], "q-", ())
    join(-1, HALVES[0])
    swapped(-1)
    reduce_i(2, HALVES[0], "z+", ("z+",))
    swapped(1)
    join(1, HALVES[1])
    reduce_i(-1, HALVES[1], "z-", ("z-",))
    swapped(0)
    reduce_t(0, 1, HALVES[1], "q+", ("q+",))
    join(1, HALVES[0])
    reduce_t(1, 0, HALVES[1], "p+", ())
    reduce_i(-1, HALVES[0], "z-", ("z-",))
    join(-1, HALVES[1])
    reduce_t(-1, 0, HALVES[0], "p-", ())
    reduce_i(1, HALVES[1], "z+", ("z+",))
    reduce_t(-1, 0, HALVES[1], "p-", ("p-",))
    reduce_t(1, 0, HALVES[0], "p+", ("p+",))
    reduce_i(1, HALVES[0], "z+", ("z+",))
    join(0, HALVES[0])
    join(0, HALVES[1])
    finish_text()
    finish_image()
    assert len(net.copies) <= N_COPIES, len(net.copies)
    net.finish()


def store(image_ref, text_ref, image_out, text_out, sems):
    copies = [
        pltpu.make_async_copy(image_ref, image_out, sems.at[0]),
        pltpu.make_async_copy(text_ref, text_out, sems.at[1]),
    ]
    for copy in copies:
        copy.start()
    for copy in copies:
        copy.wait()


def local(image_feats, text_feats, image_gain, text_gain):
    vmem = pl.BlockSpec(memory_space=pltpu.VMEM)
    block = pltpu.VMEM((ROWS, WIDTH), BF16)
    flops = 6 * TOTAL * TOTAL * WIDTH
    results = pl.pallas_call(
        kernel,
        out_shape=(block, block),
        in_specs=[pl.BlockSpec(memory_space=pl.ANY)] * 4,
        out_specs=(vmem, vmem),
        scratch_shapes=[
            pltpu.VMEM((TOTAL, WIDTH), BF16),
            pltpu.VMEM((TOTAL, WIDTH), BF16),
            pltpu.VMEM((TOTAL, TOTAL), BF16),
            pltpu.VMEM((TOTAL, TOTAL), BF16),
            pltpu.VMEM((TOTAL, WIDTH), F32),
            pltpu.VMEM((TOTAL, WIDTH), F32),
            pltpu.VMEM((T_SLOTS, ROWS, WIDTH), BF16),
            pltpu.VMEM((T_SLOTS, ROWS, WIDTH), BF16),
            pltpu.VMEM((7, ROWS, WIDTH), BF16),
            pltpu.VMEM((7, ROWS, WIDTH), BF16),
            pltpu.VMEM((8, ROWS, WIDTH), BF16),
            pltpu.VMEM((8, ROWS, WIDTH), BF16),
            pltpu.VMEM((ROWS, WIDTH), F32),
            pltpu.VMEM((ROWS, 1), F32),
            pltpu.VMEM((ROWS, 1), F32),
            pltpu.VMEM((ROWS, WIDTH), F32),
            pltpu.VMEM((ROWS, 1), F32),
            pltpu.VMEM((ROWS, 1), F32),
            pltpu.VMEM((ROWS, WIDTH), BF16),
            pltpu.VMEM((ROWS, WIDTH), BF16),
            pltpu.VMEM((WIDTH,), F32),
            pltpu.VMEM((WIDTH,), F32),
            pltpu.SemaphoreType.DMA((4,)),
            pltpu.SemaphoreType.DMA((N_COPIES,)),
            pltpu.SemaphoreType.DMA((N_COPIES,)),
        ],
        compiler_params=pltpu.CompilerParams(
            collective_id=0, has_side_effects=True, vmem_limit_bytes=56 * 2**20
        ),
        cost_estimate=pl.CostEstimate(
            flops=flops, bytes_accessed=4 * ROWS * WIDTH * 2, transcendentals=TOTAL * TOTAL
        ),
    )(image_feats, text_feats, image_gain, text_gain)
    block = jax.ShapeDtypeStruct((ROWS, WIDTH), BF16)
    anywhere = pl.BlockSpec(memory_space=pl.ANY)
    return pl.pallas_call(
        store,
        out_shape=(block, block),
        in_specs=[anywhere] * 2,
        out_specs=(anywhere, anywhere),
        scratch_shapes=[pltpu.SemaphoreType.DMA((2,))],
    )(*results)


def solution(mesh):
    placed = (P(("img", "txt"), None), P(("img", "txt"), None), P(), P())
    return jax.shard_map(
        local,
        mesh=mesh,
        in_specs=placed,
        out_specs=(P(("img", "txt"), None), P(("img", "txt"), None)),
        check_vma=False,
    )
```

```python
import math

import jax
import jax.numpy as jnp
from jax import lax
from jax.experimental import pallas as pl
from jax.experimental.pallas import tpu as pltpu
from jax.sharding import PartitionSpec as P

MESH = pl.DeviceIdType.MESH
EPSILON = 1e-06
BIAS_VALUE = -8.0
ROWS = 80
WIDTH = 1152
TOTAL = 16 * ROWS
SCALE = 2.0 * math.sqrt(WIDTH)
LOG2E = math.log2(math.e)
TILE = 256
F32 = jnp.float32
BF16 = jnp.bfloat16

HALVES = ((0, 48), (48, 32))

T_ORDER = [(dp, dq) for dq in (0, 1, 3, 2) for dp in (0, 1, 3, 2)]
Z_ORDER = (0, 1, -1, 2, -2, 3, -3, 4)


def t_row(dp, dq):
    return T_ORDER.index((dp % 4, dq % 4)) * ROWS


def wrap_z(dz):
    return (dz + 3) % 8 - 3


def i_row(dz, dc):
    return (2 * Z_ORDER.index(wrap_z(dz)) + dc) * ROWS


def mean(values):
    return jnp.sum(values, axis=-1, keepdims=True) * (1.0 / WIDTH)


def embed(feats_ref, gain_ref, normed_ref, r1_ref, r2_ref):
    feats = feats_ref[...].astype(F32)
    centre = feats - mean(feats)
    r1 = lax.rsqrt(mean(centre * centre) + EPSILON)
    normed = centre * r1
    scaled = normed * gain_ref[...]
    r2 = lax.rsqrt(mean(scaled * scaled) + EPSILON)
    normed_ref[...] = normed
    r1_ref[...] = r1
    r2_ref[...] = r2
    return (scaled * (r2 * (1.0 / math.sqrt(WIDTH)))).astype(BF16)


def embed_back(cot, gain_ref, normed_ref, r1_ref, r2_ref):
    normed, r1, r2, gain = normed_ref[...], r1_ref[...], r2_ref[...], gain_ref[...]
    scaled = normed * gain
    d_scaled = (cot - scaled * (r2 * r2 * mean(cot * scaled))) * (r2 * (1.0 / math.sqrt(WIDTH)))
    d_normed = d_scaled * gain
    d_centre = (d_normed - normed * mean(d_normed * normed)) * r1
    return (d_centre - mean(d_centre)).astype(BF16)


class Net:
    def __init__(self, send_sems, recv_sems):
        self.send_sems, self.recv_sems = send_sems, recv_sems
        self.copies = {}
        i, t = lax.axis_index("img"), lax.axis_index("txt")
        c, y, x = i % 2, (i // 2) % 4, t // 2
        z = (i // 8) * 2 + t % 2

        def place(x, y, z, c):
            x, y, z = (x + 4) % 4, (y + 4) % 4, (z + 8) % 8
            return (((z // 2) * 4 + y) * 2 + c, x * 2 + z % 2)

        s = 1 - 2 * c
        self.device = {
            "p+": place(x + (1 - c), y + c, z, c),
            "p-": place(x - (1 - c), y - c, z, c),
            "q+": place(x + c, y + (1 - c), z, c),
            "q-": place(x - c, y - (1 - c), z, c),
            "z+": place(x, y, z + s, c),
            "z-": place(x, y, z - s, c),
            "c": place(x, y, z, 1 - c),
        }

    def greet(self):
        barrier = pltpu.get_barrier_semaphore()
        for device in self.device.values():
            pl.semaphore_signal(barrier, inc=1, device_id=device, device_id_type=MESH)

    def greeted(self):
        pl.semaphore_wait(pltpu.get_barrier_semaphore(), len(self.device))

    def send(self, key, src, dst, way):
        number = len(self.copies)
        assert key not in self.copies
        copy = pltpu.make_async_remote_copy(
            src_ref=src,
            dst_ref=dst,
            send_sem=self.send_sems.at[number],
            recv_sem=self.recv_sems.at[number],
            device_id=self.device[way],
            device_id_type=MESH,
        )
        copy.start()
        self.copies[key] = copy

    def arrived(self, key):
        self.copies[key].wait_recv()

    def finish(self):
        for copy in self.copies.values():
            copy.wait_send()


N_COPIES = 111
T_SLOTS = 16
I_SLOTS = 16


def kernel(
    image_ref, text_ref, image_gain_ref, text_gain_ref, image_out, text_out,
    tbuf, ibuf, w, wt, dtext, dimage, tsend, trecv, isend, irecv, csend, crecv,
    inorm, ir1, ir2, tnorm, tr1, tr2, image_in, text_in, image_gain_in, text_gain_in, in_sems,
    send_sems, recv_sems,
):
    net = Net(send_sems, recv_sems)
    staged = [
        pltpu.make_async_copy(source, target, in_sems.at[k])
        for k, (source, target) in enumerate(
            (
                (image_ref, image_in),
                (image_gain_ref, image_gain_in),
                (text_ref, text_in),
                (text_gain_ref, text_gain_in),
            )
        )
    ]
    for copy in staged:
        copy.start()
    net.greet()

    def send_t(dp, dq, part, way):
        first, size = part
        step = 1 if way[1] == "+" else -1
        there = (dp - step, dq) if way[0] == "p" else (dp, dq - step)
        there = (there[0] % 4, there[1] % 4)
        net.send(
            ("tg", there, first),
            tbuf.at[pl.ds(t_row(dp, dq) + first, size)],
            tbuf.at[pl.ds(t_row(*there) + first, size)],
            way,
        )

    def wait_t(dp, dq, part):
        net.arrived(("tg", (dp % 4, dq % 4), part[0]))

    def send_z(dz, part, way):
        first, size = part
        there = wrap_z(dz - 1 if way == "z+" else dz + 1)
        net.send(
            ("ig", there, 0, first),
            ibuf.at[pl.ds(i_row(dz, 0) + first, size)],
            ibuf.at[pl.ds(i_row(there, 0) + first, size)],
            way,
        )

    def send_c(dz, part):
        first, size = part
        there = wrap_z(-dz)
        net.send(
            ("ig", there, 1, first),
            ibuf.at[pl.ds(i_row(dz, 0) + first, size)],
            ibuf.at[pl.ds(i_row(there, 1) + first, size)],
            "c",
        )

    def wait_i(dz, dc, part):
        net.arrived(("ig", dz, dc, part[0]))

    def tile(first_t, count_t, first_i, count_i):
        ts, im = pl.ds(first_t, count_t), pl.ds(first_i, count_i)
        dots = lax.dot_general(
            tbuf[ts, :], ibuf[im, :], (((1,), (1,)), ((), ())), preferred_element_type=F32
        )
        weights = SCALE / (1.0 + jnp.exp2(dots * (-SCALE * LOG2E) - BIAS_VALUE * LOG2E))
        if first_t == 0 and first_i == 0:
            row = lax.broadcasted_iota(jnp.int32, weights.shape, 0)
            column = lax.broadcasted_iota(jnp.int32, weights.shape, 1)
            weights = weights - jnp.where((row == column) & (row < ROWS), SCALE, 0.0)
        weights = weights.astype(BF16)
        w[ts, im] = weights
        wt[im, ts] = weights.T

    def text_rows(first, count, first_k=0, count_k=TOTAL, add=False):
        rows, ks = pl.ds(first, count), pl.ds(first_k, count_k)
        part = jnp.dot(w[rows, ks], ibuf[ks, :], preferred_element_type=F32)
        dtext[rows, :] = dtext[rows, :] + part if add else part

    def image_rows(first, count, first_k=0, count_k=TOTAL, add=False):
        rows, ks = pl.ds(first, count), pl.ds(first_k, count_k)
        part = jnp.dot(wt[rows, ks], tbuf[ks, :], preferred_element_type=F32)
        dimage[rows, :] = dimage[rows, :] + part if add else part

    whole = (0, ROWS)

    def own_image():
        staged[0].wait()
        staged[1].wait()
        ibuf[0:ROWS, :] = embed(image_in, image_gain_in, inorm, ir1, ir2)
        net.greeted()
        for part in HALVES:
            for way in ("z+", "z-"):
                send_z(0, part, way)
        send_c(0, whole)

    def own_text():
        staged[2].wait()
        staged[3].wait()
        tbuf[0:ROWS, :] = embed(text_in, text_gain_in, tnorm, tr1, tr2)
        for ways in (("p+", "p-"), ("q+", "q-")):
            for part in HALVES:
                for way in ways:
                    send_t(0, 0, part, way)

    def hop_image(dz, k):
        part = HALVES[k]
        wait_i(dz, 0, part)
        if dz in (-1, -2, -3):
            send_z(dz, part, "z+")
        if dz in (1, 2):
            send_z(dz, part, "z-")
        send_c(dz, part)

    def hop_text(dp, dq, k):
        part = HALVES[k]
        wait_t(dp, dq, part)
        if dq == 0:
            if dp == -1 and k == 0:
                send_t(dp, dq, part, "p+")
            if dp == 1 and k == 1:
                send_t(dp, dq, part, "p-")
            send_t(dp, dq, part, "q+")
            send_t(dp, dq, part, "q-")
        elif dq == -1 and dp in (0, 1):
            send_t(dp, dq, part, "q+")
        elif dq == 1 and dp in (-1, 2):
            send_t(dp, dq, part, "q-")

    slots = {}

    def slot(kind, key):
        group = slots.setdefault(kind, {})
        return group.setdefault(key, len(group))

    def reduce_t(dp, dq, part, way, takes):
        first, size = part
        step = 1 if way[1] == "+" else -1
        there = (dp - step, dq) if way[0] == "p" else (dp, dq - step)
        key = (there[0] % 4, there[1] % 4, way)
        total = dtext[pl.ds(t_row(dp, dq) + first, size), :]
        total = taken_t(total, dp, dq, part, takes)
        out = tsend.at[slot("t", key), pl.ds(first, size)]
        out[...] = total.astype(BF16)
        net.send(("tr", key, first), out, trecv.at[slot("t", key), pl.ds(first, size)], way)

    def taken_t(total, dp, dq, part, takes):
        first, size = part
        for way in takes:
            key = (dp % 4, dq % 4, way)
            net.arrived(("tr", key, first))
            total = total + trecv[slot("t", key), pl.ds(first, size), :].astype(F32)
        return total

    def swap(dz):
        out = csend.at[Z_ORDER.index(dz)]
        out[...] = dimage[pl.ds(i_row(dz, 1), ROWS), :].astype(BF16)
        there = Z_ORDER.index(wrap_z(-dz))
        net.send(("cr", wrap_z(-dz)), out, crecv.at[there], "c")

    def swapped(dz):
        net.arrived(("cr", dz))
        rows = pl.ds(i_row(dz, 0), ROWS)
        dimage[rows, :] = dimage[rows, :] + crecv[Z_ORDER.index(dz)].astype(F32)

    def taken_i(total, dz, part, takes):
        first, size = part
        for way in takes:
            key = (dz, way)
            net.arrived(("ir", key, first))
            total = total + irecv[slot("i", key), pl.ds(first, size), :].astype(F32)
        return total

    def reduce_i(dz, part, way, takes):
        first, size = part
        total = taken_i(dimage[pl.ds(i_row(dz, 0) + first, size), :], dz, part, takes)
        key = (wrap_z(dz - 1 if way == "z+" else dz + 1), way)
        out = isend.at[slot("i", key), pl.ds(first, size)]
        out[...] = total.astype(BF16)
        net.send(("ir", key, first), out, irecv.at[slot("i", key), pl.ds(first, size)], way)

    def join(dp, part):
        first, size = part
        rows = pl.ds(t_row(dp, 0) + first, size)
        dtext[rows, :] = taken_t(dtext[rows, :], dp, 0, part, ("q+", "q-"))

    def finish_text():
        total = dtext[0:ROWS, :]
        sums = [
            taken_t(total[first : first + size], 0, 0, (first, size), ("p+", "p-"))
            for first, size in HALVES
        ]
        text_out[...] = embed_back(
            jnp.concatenate(sums, axis=0), text_gain_in, tnorm, tr1, tr2
        )

    def finish_image():
        total = dimage[0:ROWS, :]
        sums = [
            taken_i(total[first : first + size], 0, (first, size), ("z-", "z+"))
            for first, size in HALVES
        ]
        image_out[...] = embed_back(
            jnp.concatenate(sums, axis=0), image_gain_in, inorm, ir1, ir2
        )

    own_image()
    own_text()
    wait_i(0, 1, whole)
    hop_image(-1, 0)
    hop_text(-1, 0, 0)
    hop_text(1, 0, 0)
    hop_image(1, 0)
    hop_text(1, 0, 1)
    hop_text(-1, 0, 1)
    wait_i(1, 1, HALVES[0])
    hop_image(-1, 1)
    hop_image(1, 1)
    hop_text(0, -1, 0)
    hop_text(0, 1, 0)
    wait_i(-1, 1, HALVES[0])
    hop_text(0, -1, 1)
    hop_text(0, 1, 1)
    wait_i(1, 1, HALVES[1])
    hop_image(-2, 0)
    wait_i(-1, 1, HALVES[1])
    hop_text(2, 0, 0)
    hop_text(-1, 1, 0)
    hop_image(2, 0)
    wait_i(2, 1, HALVES[0])
    hop_image(-2, 1)
    hop_text(-1, -1, 0)
    hop_text(1, 1, 0)
    hop_image(2, 1)
    hop_text(2, 0, 1)
    tile(0, 256, 256, 256)
    hop_text(1, -1, 0)
    wait_i(-2, 1, HALVES[0])
    tile(0, 256, 0, 256)
    hop_text(1, 1, 1)
    wait_i(2, 1, HALVES[1])
    hop_text(1, -1, 1)
    hop_image(-3, 0)
    hop_text(-1, 1, 1)
    tile(256, 256, 256, 256)
    wait_i(-2, 1, HALVES[1])
    tile(256, 256, 512, 256)
    tile(256, 256, 0, 256)
    hop_image(3, 0)
    hop_text(-1, -1, 1)
    tile(0, 256, 512, 256)
    hop_text(2, 1, 0)
    wait_i(3, 1, HALVES[0])
    hop_text(0, 2, 0)
    hop_image(-3, 1)
    hop_text(-1, 2, 0)
    hop_text(0, 2, 1)
    hop_image(3, 1)
    wait_i(-3, 1, HALVES[0])
    hop_text(2, 1, 1)
    wait_i(3, 1, HALVES[1])
    tile(256, 256, 768, 256)
    hop_text(2, -1, 0)
    tile(0, 256, 768, 256)
    hop_image(4, 0)
    hop_text(-1, 2, 1)
    wait_i(-3, 1, HALVES[1])
    hop_text(2, -1, 1)
    tile(512, 384, 256, 256)
    tile(512, 384, 0, 256)
    tile(512, 384, 768, 256)
    hop_image(4, 1)
    tile(512, 384, 512, 256)
    hop_text(1, 2, 0)
    wait_i(4, 1, HALVES[0])
    hop_text(2, 2, 0)
    hop_text(1, 2, 1)
    hop_text(2, 2, 1)
    tile(896, 384, 256, 256)
    tile(896, 384, 0, 256)
    tile(896, 384, 768, 256)
    tile(896, 384, 512, 256)
    wait_i(4, 1, HALVES[1])
    tile(256, 256, 1024, 256)
    tile(896, 384, 1024, 256)
    tile(512, 384, 1024, 256)
    tile(0, 256, 1024, 256)
    image_rows(1120, 160)
    swap(4)
    text_rows(960, 320)
    reduce_t(-1, 2, HALVES[0], "q-", ())
    reduce_t(-1, 2, HALVES[1], "q-", ())
    reduce_t(1, 2, HALVES[0], "q-", ())
    reduce_t(2, 2, HALVES[0], "q+", ())
    reduce_t(2, 2, HALVES[1], "q+", ())
    image_rows(800, 320)
    swapped(4)
    reduce_i(4, HALVES[0], "z+", ())
    swap(3)
    text_rows(320, 320)
    reduce_t(-1, 1, HALVES[0], "q+", ())
    swap(-3)
    reduce_t(1, 1, HALVES[1], "q+", ())
    reduce_i(4, HALVES[1], "z+", ())
    text_rows(640, 320)
    reduce_t(2, -1, HALVES[1], "q-", ())
    swapped(-3)
    reduce_i(-3, HALVES[1], "z-", ())
    reduce_t(2, -1, HALVES[0], "q-", ())
    reduce_t(2, 1, HALVES[0], "q+", ("q+",))
    reduce_i(-3, HALVES[0], "z-", ())
    reduce_t(1, 2, HALVES[1], "q-", ())
    image_rows(480, 320)
    swapped(3)
    reduce_i(3, HALVES[0], "z+", ("z+",))
    swap(2)
    swap(-2)
    reduce_t(2, 1, HALVES[1], "q+", ("q+",))
    reduce_t(1, 1, HALVES[0], "q+", ())
    reduce_t(1, -1, HALVES[0], "q-", ("q-",))
    image_rows(160, 320)
    reduce_i(3, HALVES[1], "z+", ("z+",))
    swap(-1)
    reduce_t(0, 2, HALVES[0], "q+", ())
    reduce_t(-1, -1, HALVES[1], "q-", ("q-",))
    reduce_t(0, 2, HALVES[1], "q+", ())
    reduce_t(-1, -1, HALVES[0], "q-", ("q-",))
    swapped(-2)
    reduce_i(-2, HALVES[1], "z-", ("z-",))
    text_rows(0, 320)
    reduce_i(-2, HALVES[0], "z-", ("z-",))
    join(2, HALVES[0])
    swapped(2)
    reduce_t(-1, 1, HALVES[1], "q+", ())
    swap(1)
    image_rows(0, 160)
    reduce_t(1, -1, HALVES[1], "q-", ("q-",))
    join(2, HALVES[1])
    reduce_i(2, HALVES[0], "z+", ("z+",))
    reduce_t(2, 0, HALVES[0], "p+", ())
    reduce_t(2, 0, HALVES[1], "p-", ())
    reduce_t(0, -1, HALVES[1], "q-", ())
    reduce_t(0, -1, HALVES[0], "q-", ())
    swapped(1)
    swap(0)
    join(1, HALVES[0])
    reduce_i(2, HALVES[1], "z+", ("z+",))
    swapped(-1)
    reduce_i(-1, HALVES[1], "z-", ("z-",))
    reduce_t(0, 1, HALVES[0], "q+", ("q+",))
    swapped(0)
    reduce_t(0, 1, HALVES[1], "q+", ("q+",))
    join(-1, HALVES[0])
    reduce_i(-1, HALVES[0], "z-", ("z-",))
    join(-1, HALVES[1])
    reduce_t(-1, 0, HALVES[0], "p-", ())
    join(1, HALVES[1])
    reduce_t(1, 0, HALVES[1], "p+", ())
    reduce_i(1, HALVES[0], "z+", ("z+",))
    reduce_t(-1, 0, HALVES[1], "p-", ("p-",))
    reduce_t(1, 0, HALVES[0], "p+", ("p+",))
    reduce_i(1, HALVES[1], "z+", ("z+",))
    join(0, HALVES[0])
    join(0, HALVES[1])
    finish_text()
    finish_image()
    assert len(net.copies) <= N_COPIES, len(net.copies)
    net.finish()


def local(image_feats, text_feats, image_gain, text_gain):
    vmem = pl.BlockSpec(memory_space=pltpu.VMEM)
    block = pltpu.VMEM((ROWS, WIDTH), BF16)
    flops = 6 * TOTAL * TOTAL * WIDTH
    return pl.pallas_call(
        kernel,
        out_shape=(block, block),
        in_specs=[pl.BlockSpec(memory_space=pl.ANY)] * 4,
        out_specs=(vmem, vmem),
        scratch_shapes=[
            pltpu.VMEM((TOTAL, WIDTH), BF16),
            pltpu.VMEM((TOTAL, WIDTH), BF16),
            pltpu.VMEM((TOTAL, TOTAL), BF16),
            pltpu.VMEM((TOTAL, TOTAL), BF16),
            pltpu.VMEM((TOTAL, WIDTH), F32),
            pltpu.VMEM((TOTAL, WIDTH), F32),
            pltpu.VMEM((T_SLOTS, ROWS, WIDTH), BF16),
            pltpu.VMEM((T_SLOTS, ROWS, WIDTH), BF16),
            pltpu.VMEM((7, ROWS, WIDTH), BF16),
            pltpu.VMEM((7, ROWS, WIDTH), BF16),
            pltpu.VMEM((8, ROWS, WIDTH), BF16),
            pltpu.VMEM((8, ROWS, WIDTH), BF16),
            pltpu.VMEM((ROWS, WIDTH), F32),
            pltpu.VMEM((ROWS, 1), F32),
            pltpu.VMEM((ROWS, 1), F32),
            pltpu.VMEM((ROWS, WIDTH), F32),
            pltpu.VMEM((ROWS, 1), F32),
            pltpu.VMEM((ROWS, 1), F32),
            pltpu.VMEM((ROWS, WIDTH), BF16),
            pltpu.VMEM((ROWS, WIDTH), BF16),
            pltpu.VMEM((WIDTH,), F32),
            pltpu.VMEM((WIDTH,), F32),
            pltpu.SemaphoreType.DMA((4,)),
            pltpu.SemaphoreType.DMA((N_COPIES,)),
            pltpu.SemaphoreType.DMA((N_COPIES,)),
        ],
        compiler_params=pltpu.CompilerParams(
            collective_id=0, has_side_effects=True, vmem_limit_bytes=56 * 2**20
        ),
        cost_estimate=pl.CostEstimate(
            flops=flops, bytes_accessed=4 * ROWS * WIDTH * 2, transcendentals=TOTAL * TOTAL
        ),
    )(image_feats, text_feats, image_gain, text_gain)


def solution(mesh):
    placed = (P(("img", "txt"), None), P(("img", "txt"), None), P(), P())
    return jax.shard_map(
        local,
        mesh=mesh,
        in_specs=placed,
        out_specs=(P(("img", "txt"), None), P(("img", "txt"), None)),
        check_vma=False,
    )
```
